32 devices in a mesh: lat: 4 (over y, core), lon: 8 (over z, x).
Axes of the slice: x: 2, y: 2, z: 4, core: 2. Of those that a mesh axis runs over, the one named last changes fastest.
Arguments:
- control: float32 [512, 1024, 128], P('lat', 'lon'), may hold values from -6 to 6
- corr_blocks: float32 [9, 128, 128], replicated, may hold values from -0.1875 to 0.1875
- jacobian: float32 [128, 128], replicated, may hold values from -0.5 to 0.5
- obs_values: bfloat16 [65536, 128], P(('lat', 'lon')), may hold values from -6 to 6
- obs_count: int32 [32, 32], P(('lat', 'lon')), may hold values from 16 to 64, as said below
- obs_col: int32 [32, 2048], P(('lat', 'lon')), may hold values from 0 to 16254, as said below
- obs_frac: float32 [32, 2, 2048], P(('lat', 'lon')), may hold values from 0 to 1
- obs_rinv: float32 [32, 2048], P(('lat', 'lon')), may hold values from 0.25 to 4
Outputs:
- gradient: float32 [512, 1024, 128], P('lat', 'lon')
- weighted_dep: bfloat16 [65536, 128], P(('lat', 'lon'))
The draws below stay inside these ranges and needn't reach their ends.
Inputs may be any that keep to these rules, and one draw needn't show every extreme that they name: `obs_count`: every source fills all 64 slots for at least one owner, and one owner receives 64 from every source. `obs_col`: i * 128 + j with i < 127 and j < 127, so the 2 x 2 stencil lies in the owner's block; entries of dead slots are valid too.
All inputs are finite; a program needn't handle non-finite values.
Results may differ from the reference program's by a relative error of at most 0.001.
Values may be sent and summed in bfloat16 or wider, within the bound.
A program may use at most 192 MiB of HBM per device.

```python
import math
import jax
import jax.numpy as jnp
from jax import lax

CLAT = 128
CLON = 128
LEV = 128
CH = 128
CAP = 64
NLAT = 512
NLON = 1024
SLOTS = 2048
N_LAT = 4
N_LON = 8
DEVICES = 32


def draw_obs_count(key, part):
    key_busy, key_quiet, key_heavy, key_hot = jax.random.split(key, 4)
    busy = jax.random.randint(key_busy, (DEVICES, 1), 0, 4) == 0
    quiet = jax.random.randint(key_quiet, (DEVICES, DEVICES), CAP // 4, 3 * CAP // 4 + 1)
    heavy = CAP - jax.random.randint(key_heavy, (DEVICES, DEVICES), 0, CAP // 4 + 1)
    counts = jnp.where(busy, heavy, quiet)
    hot_row = jax.random.randint(key_hot, (), 0, DEVICES)
    row_ids = jnp.arange(DEVICES)[:, None]
    return jnp.where(row_ids == hot_row, CAP, counts).astype(jnp.int32)


def draw_obs_col(key, part):
    key_lat, key_lon = jax.random.split(key, 2)
    lat_pick = jax.random.randint(key_lat, (DEVICES, DEVICES * CAP), 0, CLAT - 1)
    lon_pick = jax.random.randint(key_lon, (DEVICES, DEVICES * CAP), 0, CLON - 1)
    corners = lat_pick * CLON + lon_pick
    corners = corners.at[0, 0].set((CLAT - 2) * CLON + CLON - 2)
    corners = corners.at[0, 1].set(0)
    return corners.astype(jnp.int32)


def block_levels(key, dims, shards, least, largest):
    gain = 1.0
    for dim, shards_of in shards:
        heights = jax.random.uniform(jax.random.fold_in(jax.random.fold_in(key, 6), dim), (shards_of,), jnp.float32, least / len(shards), largest / len(shards))
        gain = gain * jnp.repeat(jnp.exp(heights), dims[dim] // shards_of).reshape((-1,) + (1,) * (len(dims) - 1 - dim))
    return gain


def noise(own_key, dims, deviation, reach, pieces=(), kind=jnp.bfloat16):
    result = deviation * jax.random.normal(own_key, dims, jnp.float32)
    if pieces:
        result = result * block_levels(own_key, dims, pieces, -0.22, 0.18)
    return jnp.clip(result, -reach, reach).astype(kind)


def setup_inputs(seed: int = 0) -> dict:
    key_list = jax.random.split(jax.random.key(seed), 9)
    control = noise(key_list[0], (NLAT, NLON, LEV), 1.0, 6.0, ((0, 4), (1, 8)), jnp.float32)
    corr_blocks = noise(key_list[1], (9, LEV, LEV), (9 * LEV) ** -0.5, 0.1875, (), jnp.float32)
    jacobian = noise(key_list[2], (LEV, CH), LEV ** -0.5, 0.5, (), jnp.float32)
    obs_values = noise(key_list[3], (DEVICES * DEVICES * CAP, CH), 1.0, 6.0, ((0, 32),))
    obs_count = draw_obs_count(jax.random.fold_in(key_list[8], 71), 0)
    obs_col = draw_obs_col(jax.random.fold_in(key_list[8], 71), 0)
    obs_frac = jnp.clip(1.0 * jax.random.uniform(key_list[6], (DEVICES, 2, SLOTS), jnp.float32) ** block_levels(key_list[6], (DEVICES, 2, SLOTS), ((0, 32),), -0.2, 0.2), 0.0, 1.0)
    obs_rinv = jnp.clip(jnp.exp(math.log(4.0) - 2.7725887 * jax.random.uniform(key_list[7], (DEVICES, SLOTS), jnp.float32) ** block_levels(key_list[7], (DEVICES, SLOTS), ((0, 32),), -0.2, 0.2)), 0.25, 4.0)
    return {"control": control, "corr_blocks": corr_blocks, "jacobian": jacobian, "obs_values": obs_values, "obs_count": obs_count, "obs_col": obs_col, "obs_frac": obs_frac, "obs_rinv": obs_rinv}


def apply_root(padded, corr_blocks):
    height = padded.shape[0] - 2
    breadth = padded.shape[1] - 2
    summed = jnp.zeros((height, breadth, corr_blocks.shape[2]), jnp.float32)
    for step_lat in (-1, 0, 1):
        for step_lon in (-1, 0, 1):
            which = (step_lat + 1) * 3 + (step_lon + 1)
            piece = padded[1 + step_lat:1 + step_lat + height, 1 + step_lon:1 + step_lon + breadth]
            summed = summed + jnp.einsum('ijl,lm->ijm', piece, corr_blocks[which], precision=lax.Precision.HIGHEST)
    return summed


def apply_transpose(padded, corr_blocks):
    height = padded.shape[0] - 2
    breadth = padded.shape[1] - 2
    summed = jnp.zeros((height, breadth, corr_blocks.shape[1]), jnp.float32)
    for step_lat in (-1, 0, 1):
        for step_lon in (-1, 0, 1):
            which = (step_lat + 1) * 3 + (step_lon + 1)
            piece = padded[1 - step_lat:1 - step_lat + height, 1 - step_lon:1 - step_lon + breadth]
            summed = summed + jnp.einsum('ijm,lm->ijl', piece, corr_blocks[which], precision=lax.Precision.HIGHEST)
    return summed


def observe(state_rows, observed, counts, corners, fractions, rinv, jacobian):
    frac_lat = fractions[0][:, None]
    frac_lon = fractions[1][:, None]
    weight_sw = (1.0 - frac_lat) * (1.0 - frac_lon)
    weight_se = (1.0 - frac_lat) * frac_lon
    weight_nw = frac_lat * (1.0 - frac_lon)
    weight_ne = frac_lat * frac_lon
    profile = (weight_sw * jnp.take(state_rows, corners, axis=0)
               + weight_se * jnp.take(state_rows, corners + 1, axis=0)
               + weight_nw * jnp.take(state_rows, corners + CLON, axis=0)
               + weight_ne * jnp.take(state_rows, corners + CLON + 1, axis=0))
    evolved = jnp.dot(profile, jacobian, precision=lax.Precision.HIGHEST)
    departure = evolved - observed.astype(jnp.float32)
    live_slot = (jnp.arange(CAP, dtype=jnp.int32)[None, :] < counts[:, None]).reshape(-1)
    weighted = jnp.where(live_slot[:, None], rinv[:, None] * departure, jnp.zeros_like(departure))
    adjoint_rows = jnp.dot(weighted, jacobian.T, precision=lax.Precision.HIGHEST)
    targets = jnp.concatenate([corners, corners + 1, corners + CLON, corners + CLON + 1])
    spread_terms = jnp.concatenate([weight_sw * adjoint_rows, weight_se * adjoint_rows,
                                    weight_nw * adjoint_rows, weight_ne * adjoint_rows], axis=0)
    increment = jax.ops.segment_sum(spread_terms, targets, num_segments=state_rows.shape[0])
    return weighted, increment


def reference(control, corr_blocks, jacobian, obs_values, obs_count, obs_col, obs_frac, obs_rinv):
    padded = jnp.pad(control, ((1, 1), (1, 1), (0, 0)))
    state = apply_root(padded, corr_blocks)
    grouped = obs_values.reshape(DEVICES, DEVICES, CAP, CH)

    def per_owner(owner):
        lat_index = (owner // N_LON).astype(jnp.int32)
        lon_index = (owner % N_LON).astype(jnp.int32)
        zero_start = jnp.zeros((), jnp.int32)
        local_state = lax.dynamic_slice(state, (lat_index * CLAT, lon_index * CLON, zero_start), (CLAT, CLON, LEV))
        observed = lax.dynamic_index_in_dim(grouped, owner, 1, keepdims=False).reshape(DEVICES * CAP, CH)
        return observe(local_state.reshape(CLAT * CLON, LEV), observed, obs_count[owner], obs_col[owner],
                       obs_frac[owner], obs_rinv[owner], jacobian)

    weighted, increment = lax.map(per_owner, jnp.arange(DEVICES, dtype=jnp.int32))
    increment = increment.reshape(N_LAT, N_LON, CLAT, CLON, LEV).transpose(0, 2, 1, 3, 4)
    increment = increment.reshape(N_LAT * CLAT, N_LON * CLON, LEV)
    gradient = control + apply_transpose(jnp.pad(increment, ((1, 1), (1, 1), (0, 0))), corr_blocks)
    weighted_dep = weighted.reshape(DEVICES, DEVICES, CAP, CH).transpose(1, 0, 2, 3).reshape(DEVICES * DEVICES * CAP, CH)
    return gradient, weighted_dep.astype(jnp.bfloat16)
```

```python
import functools
import jax
import jax.numpy as jnp
from jax import lax
from jax.experimental import pallas as pl
from jax.experimental.pallas import tpu as pltpu
from jax.sharding import PartitionSpec as P

CAP = 64
CS = 128
EDGE = 8
F32 = jnp.float32
BF16 = jnp.bfloat16
UNROLL = 8


def split(x):
    hi = x.astype(BF16)
    return hi, (x - hi.astype(F32)).astype(BF16)


def column(row):
    return jnp.broadcast_to(row, (128, CS)).T


def combined(corr_ref, jac_ref, k):
    return jnp.dot(corr_ref[k], jac_ref[...], precision=lax.Precision.HIGHEST, preferred_element_type=F32)


def forward_kernel(pitch, col_ref, frac_ref, corr_ref, jac_ref, north_ref, south_ref, west_ref, east_ref, control_ref,
                   out_ref, pad, planes, p_hi, p_lo, g_both, sem):
    rows, cols, _ = control_ref.shape
    fetch = pltpu.make_async_copy(control_ref, pad.at[pl.ds(1, rows), pl.ds(EDGE, cols), :], sem)
    fetch.start()
    for k in range(9):
        hi, lo = split(combined(corr_ref, jac_ref, k))
        g_both[k * 128:(k + 1) * 128, 0:128] = hi
        g_both[k * 128:(k + 1) * 128, 128:256] = lo
    pad[0, EDGE:EDGE + cols, :] = north_ref[...]
    pad[rows + 1, EDGE:EDGE + cols, :] = south_ref[...]
    for side, at in ((west_ref, EDGE - 1), (east_ref, EDGE + cols)):
        def put(i, c, side=side, at=at):
            pad[pl.ds(i, 1), at:at + 1, :] = side[pl.ds(i, 1), :].reshape(1, 1, 128)
            return c
        lax.fori_loop(0, rows + 2, put, 0)
    fetch.wait()
    flat = pad.reshape((rows + 2) * pitch, 128)

    def chunk(n, carry):
        first = n * CS

        def pick(t, c):
            for v in range(UNROLL):
                s = t * UNROLL + v
                corner = col_ref[0, first + s]
                base = corner + (corner // cols) * (pitch - cols) + (EDGE - 1)
                for r in range(4):
                    planes[pl.ds(r * 4 * CS + s, 4, stride=CS), :] = flat[pl.ds(base + r * pitch, 4), :]
            return c

        lax.fori_loop(0, CS // UNROLL, pick, 0)
        at = pl.ds(pl.multiple_of(first, CS), CS)
        f = column(frac_ref[0, 0:1, at])
        g = column(frac_ref[0, 1:2, at])
        for a in range(3):
            lat = []
            for q in range(4):
                low = planes[(a * 4 + q) * CS:(a * 4 + q + 1) * CS, :]
                high = planes[((a + 1) * 4 + q) * CS:((a + 1) * 4 + q + 1) * CS, :]
                lat.append((1.0 - f) * low + f * high)
            for b in range(3):
                hi, lo = split((1.0 - g) * lat[b] + g * lat[b + 1])
                k = 3 * a + b
                p_hi[:, k * 128:(k + 1) * 128] = hi
                p_lo[:, k * 128:(k + 1) * 128] = lo
        both = jnp.dot(p_hi[...], g_both[...], preferred_element_type=F32)
        both += jnp.dot(p_lo[...], g_both[...], preferred_element_type=F32)
        out_ref[at, :] = both[:, 0:128] + both[:, 128:256]
        return carry

    lax.fori_loop(0, col_ref.shape[1] // CS, chunk, 0)


def adjoint_kernel(pitch, col_ref, frac_ref, corr_ref, jac_ref, weighted_ref, control_ref,
                   grad_ref, north_ref, south_ref, west_ref, east_ref, pad, planes, q_ref, gt_hi, gt_lo, sem):
    rows, cols, _ = control_ref.shape
    inner = pad.at[pl.ds(1, rows), pl.ds(EDGE, cols), :]
    fetch = pltpu.make_async_copy(control_ref, inner, sem)
    fetch.start()
    for k in range(9):
        hi, lo = split(combined(corr_ref, jac_ref, k).T)
        for half in range(2):
            gt_hi[half * 128:(half + 1) * 128, k * 128:(k + 1) * 128] = hi
            gt_lo[half * 128:(half + 1) * 128, k * 128:(k + 1) * 128] = lo
    for i in (0, rows + 1):
        pad[i] = jnp.zeros((pitch, 128), F32)

    def clear(i, c):
        pad[pl.ds(i, 1), 0:EDGE, :] = jnp.zeros((1, EDGE, 128), F32)
        pad[pl.ds(i, 1), EDGE + cols:pitch, :] = jnp.zeros((1, pitch - cols - EDGE, 128), F32)
        return c

    lax.fori_loop(1, rows + 1, clear, 0)
    fetch.wait()
    flat = pad.reshape((rows + 2) * pitch, 128)

    def chunk(n, carry):
        first = n * CS
        at = pl.ds(pl.multiple_of(first, CS), CS)
        w_hi, w_lo = split(weighted_ref[at, :])
        w = jnp.concatenate([w_hi, w_lo], axis=1)
        q_ref[...] = (jnp.dot(w, gt_hi[...], preferred_element_type=F32)
                      + jnp.dot(w, gt_lo[...], preferred_element_type=F32))
        f = column(frac_ref[0, 0:1, at])
        g = column(frac_ref[0, 1:2, at])
        for c in range(4):
            line = []
            for a in range(3):
                part = None
                if c < 3:
                    part = (1.0 - g) * q_ref[:, (3 * a + c) * 128:(3 * a + c + 1) * 128]
                if c > 0:
                    other = g * q_ref[:, (3 * a + c - 1) * 128:(3 * a + c) * 128]
                    part = other if part is None else part + other
                line.append(part)
            for r in range(4):
                part = None
                if r < 3:
                    part = (1.0 - f) * line[r]
                if r > 0:
                    other = f * line[r - 1]
                    part = other if part is None else part + other
                planes[(r * 4 + c) * CS:(r * 4 + c + 1) * CS, :] = part

        def spread(t, c):
            for v in range(UNROLL):
                s = t * UNROLL + v
                corner = col_ref[0, first + s]
                base = corner + (corner // cols) * (pitch - cols) + (EDGE - 1)
                for r in range(4):
                    flat[pl.ds(base + r * pitch, 4), :] += planes[pl.ds(r * 4 * CS + s, 4, stride=CS), :]
            return c

        lax.fori_loop(0, CS // UNROLL, spread, 0)
        return carry

    lax.fori_loop(0, col_ref.shape[1] // CS, chunk, 0)
    send = pltpu.make_async_copy(inner, grad_ref, sem)
    send.start()
    north_ref[...] = pad[0]
    south_ref[...] = pad[rows + 1]
    west_ref[...] = flat[pl.ds(pitch + EDGE - 1, rows, stride=pitch), :]
    east_ref[...] = flat[pl.ds(pitch + EDGE + cols, rows, stride=pitch), :]
    send.wait()


def finish_kernel(north_ref, south_ref, west_ref, east_ref, nw_ref, ne_ref, sw_ref, se_ref, grad_in,
                  grad_ref, line_n, line_s, tile_w, tile_e, sems):
    rows, cols, _ = grad_in.shape
    inner = pl.ds(1, rows - 2)
    ends = ((grad_ref.at[0], line_n), (grad_ref.at[rows - 1], line_s),
            (grad_ref.at[inner, pl.ds(0, 8), :], tile_w), (grad_ref.at[inner, pl.ds(cols - 8, 8), :], tile_e))
    loads = [pltpu.make_async_copy(far, near, sems.at[i]) for i, (far, near) in enumerate(ends)]
    for copy in loads:
        copy.start()
    for copy in loads:
        copy.wait()
    line_n[...] += north_ref[...]
    line_s[...] += south_ref[...]
    line_n[0:1, :] += west_ref[0:1, :] + nw_ref[...]
    line_n[cols - 1:cols, :] += east_ref[0:1, :] + ne_ref[...]
    line_s[0:1, :] += west_ref[rows - 1:rows, :] + sw_ref[...]
    line_s[cols - 1:cols, :] += east_ref[rows - 1:rows, :] + se_ref[...]

    flat_w = tile_w.reshape((rows - 2) * 8, 128)
    flat_e = tile_e.reshape((rows - 2) * 8, 128)
    flat_w[pl.ds(0, rows - 2, stride=8), :] += west_ref[1:rows - 1, :]
    flat_e[pl.ds(7, rows - 2, stride=8), :] += east_ref[1:rows - 1, :]
    stores = [pltpu.make_async_copy(near, far, sems.at[i]) for i, (far, near) in enumerate(ends)]
    for copy in stores:
        copy.start()
    for copy in stores:
        copy.wait()


def shift(x, d_lat, d_lon):
    n_lat, n_lon = lax.axis_size("lat"), lax.axis_size("lon")
    pairs = []
    for p in range(n_lat):
        for q in range(n_lon):
            to_p, to_q = p + d_lat, q + d_lon
            if 0 <= to_p < n_lat and 0 <= to_q < n_lon:
                pairs.append((p * n_lon + q, to_p * n_lon + to_q))
    return lax.ppermute(x, ("lat", "lon"), pairs)


def body(control, corr_blocks, jacobian, obs_values, obs_count, obs_col, obs_frac, obs_rinv):
    n_devices = lax.axis_size("lat") * lax.axis_size("lon")
    rows, cols, levels = control.shape
    channels = jacobian.shape[1]
    slots = obs_col.shape[1]
    pitch = cols + 2 * EDGE
    vmem = pl.BlockSpec(memory_space=pltpu.VMEM)
    smem = pl.BlockSpec(memory_space=pltpu.SMEM)
    hbm = pl.BlockSpec(memory_space=pl.ANY)

    incoming = lax.all_to_all(obs_values.reshape(n_devices, CAP, channels), ("lat", "lon"),
                              split_axis=0, concat_axis=0, tiled=True)
    north = shift(control[rows - 1], 1, 0)
    south = shift(control[0], -1, 0)
    west = shift(control[:, cols - 1], 0, 1)
    east = shift(control[:, 0], 0, -1)
    nw = shift(control[rows - 1, cols - 1:], 1, 1)
    ne = shift(control[rows - 1, :1], 1, -1)
    sw = shift(control[0, cols - 1:], -1, 1)
    se = shift(control[0, :1], -1, -1)
    west = jnp.concatenate([nw, west, sw])
    east = jnp.concatenate([ne, east, se])

    limit = pltpu.CompilerParams(vmem_limit_bytes=40 * 2**20)
    evolved = pl.pallas_call(
        functools.partial(forward_kernel, pitch),
        out_shape=jax.ShapeDtypeStruct((slots, channels), F32),
        in_specs=[smem] + [vmem] * 7 + [hbm],
        out_specs=vmem,
        scratch_shapes=[
            pltpu.VMEM((rows + 2, pitch, levels), F32),
            pltpu.VMEM((16 * CS, levels), F32),
            pltpu.VMEM((CS, 9 * levels), BF16),
            pltpu.VMEM((CS, 9 * levels), BF16),
            pltpu.VMEM((9 * levels, 2 * channels), BF16),
            pltpu.SemaphoreType.DMA,
        ],
        compiler_params=limit,
        cost_estimate=pl.CostEstimate(flops=2 * slots * 1152 * 512, bytes_accessed=40 * 2**20, transcendentals=0),
        name="forward",
    )(obs_col, obs_frac, corr_blocks, jacobian, north, south, west, east, control)

    departure = evolved - incoming.reshape(slots, channels).astype(F32)
    live = (jnp.arange(CAP, dtype=jnp.int32)[None, :] < obs_count[0][:, None]).reshape(slots, 1)
    weighted = jnp.where(live, obs_rinv[0][:, None] * departure, jnp.zeros_like(departure))
    returned = lax.all_to_all(weighted.astype(BF16).reshape(n_devices, CAP, channels), ("lat", "lon"),
                              split_axis=0, concat_axis=0, tiled=True)

    gradient, out_n, out_s, out_w, out_e = pl.pallas_call(
        functools.partial(adjoint_kernel, pitch),
        out_shape=[
            jax.ShapeDtypeStruct(control.shape, F32),
            jax.ShapeDtypeStruct((pitch, levels), F32),
            jax.ShapeDtypeStruct((pitch, levels), F32),
            jax.ShapeDtypeStruct((rows, levels), F32),
            jax.ShapeDtypeStruct((rows, levels), F32),
        ],
        in_specs=[smem] + [vmem] * 4 + [hbm],
        out_specs=[hbm] + [vmem] * 4,
        scratch_shapes=[
            pltpu.VMEM((rows + 2, pitch, levels), F32),
            pltpu.VMEM((16 * CS, levels), F32),
            pltpu.VMEM((CS, 9 * levels), F32),
            pltpu.VMEM((2 * channels, 9 * levels), BF16),
            pltpu.VMEM((2 * channels, 9 * levels), BF16),
            pltpu.SemaphoreType.DMA,
        ],
        compiler_params=limit,
        cost_estimate=pl.CostEstimate(flops=2 * slots * 1152 * 512, bytes_accessed=60 * 2**20, transcendentals=0),
        name="adjoint",
    )(obs_col, obs_frac, corr_blocks, jacobian, weighted, control)

    got_s = shift(out_n[EDGE:EDGE + cols], -1, 0)
    got_n = shift(out_s[EDGE:EDGE + cols], 1, 0)
    got_e = shift(out_w, 0, -1)
    got_w = shift(out_e, 0, 1)
    got_se = shift(out_n[EDGE - 1:EDGE], -1, -1)
    got_sw = shift(out_n[EDGE + cols:EDGE + cols + 1], -1, 1)
    got_ne = shift(out_s[EDGE - 1:EDGE], 1, -1)
    got_nw = shift(out_s[EDGE + cols:EDGE + cols + 1], 1, 1)
    gradient = pl.pallas_call(
        finish_kernel,
        out_shape=jax.ShapeDtypeStruct(control.shape, F32),
        in_specs=[vmem] * 8 + [hbm],
        out_specs=hbm,
        scratch_shapes=[
            pltpu.VMEM((cols, levels), F32),
            pltpu.VMEM((cols, levels), F32),
            pltpu.VMEM((rows - 2, 8, levels), F32),
            pltpu.VMEM((rows - 2, 8, levels), F32),
            pltpu.SemaphoreType.DMA((4,)),
        ],
        input_output_aliases={8: 0},
        name="finish",
    )(got_n, got_s, got_w, got_e, got_nw, got_ne, got_sw, got_se, gradient)
    return (gradient, returned.reshape(n_devices * CAP, channels))


def solution(mesh):
    in_specs = (
        P("lat", "lon", None),
        P(),
        P(),
        P(("lat", "lon"), None),
        P(("lat", "lon"), None),
        P(("lat", "lon"), None),
        P(("lat", "lon"), None, None),
        P(("lat", "lon"), None),
    )
    out_specs = (P("lat", "lon", None), P(("lat", "lon"), None))
    return jax.shard_map(body, mesh=mesh, in_specs=in_specs, out_specs=out_specs, check_vma=False)
```

```python
import functools
import math
import jax
import jax.numpy as jnp
from jax import lax
from jax.experimental import pallas as pl
from jax.experimental.pallas import tpu as pltpu
from jax.sharding import PartitionSpec as P

CAP = 64
SUB = 128
ODD = 17
EDGE = 8
F32 = jnp.float32
BF16 = jnp.bfloat16
UNROLL = 8
WAYS = ((1, 0), (-1, 0), (0, 1), (0, -1), (1, 1), (1, -1), (-1, 1), (-1, -1))


def split(x):
    hi = x.astype(BF16)
    return hi, (x - hi.astype(F32)).astype(BF16)


def column(row):
    return jnp.broadcast_to(row, (128, SUB)).T


def combined(corr_ref, jac_ref, k):
    return jnp.dot(corr_ref[k], jac_ref[...], precision=lax.Precision.HIGHEST, preferred_element_type=F32)


def place(corner, cols, pitch):
    if cols & (cols - 1) == 0:
        line = lax.shift_right_logical(corner, cols.bit_length() - 1)
    else:
        line = lax.div(corner, cols)
    return corner + line * (pitch - cols) + (EDGE - 1)


def forward_kernel(pitch, chunk_slots, col_ref, frac_ref, corr_ref, jac_ref, north_ref, south_ref, west_ref, east_ref,
                   control_ref, out_ref, pad, patches, p_both, g_both, sem):
    rows, cols, _ = control_ref.shape
    fetch = pltpu.make_async_copy(control_ref, pad.at[pl.ds(1, rows), pl.ds(EDGE, cols), :], sem)
    fetch.start()
    for k in range(9):
        hi, lo = split(combined(corr_ref, jac_ref, k))
        g_both[k * 128:(k + 1) * 128, 0:128] = hi
        g_both[k * 128:(k + 1) * 128, 128:256] = lo
    flat = pad.reshape((rows + 2) * pitch, 128)
    pad[0, EDGE:EDGE + cols, :] = north_ref[...]
    pad[rows + 1, EDGE:EDGE + cols, :] = south_ref[...]
    flat[pl.ds(EDGE - 1, rows + 2, stride=pitch), :] = west_ref[EDGE - 1:EDGE + rows + 1, :]
    flat[pl.ds(EDGE + cols, rows + 2, stride=pitch), :] = east_ref[EDGE - 1:EDGE + rows + 1, :]
    fetch.wait()

    def chunk(n, carry):
        first = n * chunk_slots

        def pick(t, c):
            for v in range(UNROLL):
                s = t * UNROLL + v
                base = place(col_ref[0, first + s], cols, pitch)
                lines = [flat[pl.ds(base + r * pitch, 4), :] for r in range(4)]
                for r in range(4):
                    patches[pl.ds(s * ODD + r * 4, 4), :] = lines[r]
            return c

        lax.fori_loop(0, chunk_slots // UNROLL, pick, 0)

        def mix(m, c):
            at = pl.ds(pl.multiple_of(first + m * SUB, SUB), SUB)
            hi_at = pl.ds(pl.multiple_of(m * SUB, SUB), SUB)
            lo_at = pl.ds(pl.multiple_of(chunk_slots + m * SUB, SUB), SUB)
            f = column(frac_ref[0, 0:1, at])
            g = column(frac_ref[0, 1:2, at])
            origin = m * (SUB * ODD)
            for a in range(3):
                lat = []
                for q in range(4):
                    low = patches[pl.ds(origin + a * 4 + q, SUB, stride=ODD), :]
                    high = patches[pl.ds(origin + a * 4 + 4 + q, SUB, stride=ODD), :]
                    lat.append((1.0 - f) * low + f * high)
                for b in range(3):
                    hi, lo = split((1.0 - g) * lat[b] + g * lat[b + 1])
                    k = 3 * a + b
                    p_both[hi_at, k * 128:(k + 1) * 128] = hi
                    p_both[lo_at, k * 128:(k + 1) * 128] = lo
            return c

        lax.fori_loop(0, chunk_slots // SUB, mix, 0)
        both = jnp.dot(p_both[...], g_both[...], preferred_element_type=F32)
        hi, lo = both[0:chunk_slots], both[chunk_slots:]
        out_ref[pl.ds(pl.multiple_of(first, chunk_slots), chunk_slots), :] = (
            hi[:, 0:128] + (hi[:, 128:256] + lo[:, 0:128] + lo[:, 128:256]))
        return carry

    lax.fori_loop(0, col_ref.shape[1] // chunk_slots, chunk, 0)


def adjoint_kernel(pitch, chunk_slots, col_ref, frac_ref, corr_ref, jac_ref, weighted_ref, control_ref,
                   grad_ref, north_ref, south_ref, west_ref, east_ref, pad, patches, q_ref, gt_hi, gt_lo, sem):
    rows, cols, _ = control_ref.shape
    inner = pad.at[pl.ds(1, rows), pl.ds(EDGE, cols), :]
    fetch = pltpu.make_async_copy(control_ref, inner, sem)
    fetch.start()
    for k in range(9):
        hi, lo = split(combined(corr_ref, jac_ref, k).T)
        for half in range(2):
            gt_hi[half * 128:(half + 1) * 128, k * 128:(k + 1) * 128] = hi
            gt_lo[half * 128:(half + 1) * 128, k * 128:(k + 1) * 128] = lo
    for i in (0, rows + 1):
        pad[i] = jnp.zeros((pitch, 128), F32)

    def clear(i, c):
        pad[pl.ds(i, 1), 0:EDGE, :] = jnp.zeros((1, EDGE, 128), F32)
        pad[pl.ds(i, 1), EDGE + cols:pitch, :] = jnp.zeros((1, pitch - cols - EDGE, 128), F32)
        return c

    lax.fori_loop(1, rows + 1, clear, 0)
    fetch.wait()
    flat = pad.reshape((rows + 2) * pitch, 128)

    def chunk(n, carry):
        first = n * chunk_slots
        w_hi, w_lo = split(weighted_ref[pl.ds(pl.multiple_of(first, chunk_slots), chunk_slots), :])
        w = jnp.concatenate([w_hi, w_lo], axis=1)
        q_ref[...] = (jnp.dot(w, gt_hi[...], preferred_element_type=F32)
                      + jnp.dot(w, gt_lo[...], preferred_element_type=F32))

        def mix(m, carry):
            at = pl.ds(pl.multiple_of(first + m * SUB, SUB), SUB)
            here = pl.ds(pl.multiple_of(m * SUB, SUB), SUB)
            f = column(frac_ref[0, 0:1, at])
            g = column(frac_ref[0, 1:2, at])
            origin = m * (SUB * ODD)
            for c in range(4):
                line = []
                for a in range(3):
                    part = None
                    if c < 3:
                        part = (1.0 - g) * q_ref[here, (3 * a + c) * 128:(3 * a + c + 1) * 128]
                    if c > 0:
                        other = g * q_ref[here, (3 * a + c - 1) * 128:(3 * a + c) * 128]
                        part = other if part is None else part + other
                    line.append(part)
                for r in range(4):
                    part = None
                    if r < 3:
                        part = (1.0 - f) * line[r]
                    if r > 0:
                        other = f * line[r - 1]
                        part = other if part is None else part + other
                    patches[pl.ds(origin + r * 4 + c, SUB, stride=ODD), :] = part
            return carry

        lax.fori_loop(0, chunk_slots // SUB, mix, 0)

        def spread(t, c):
            for v in range(UNROLL):
                s = t * UNROLL + v
                base = place(col_ref[0, first + s], cols, pitch)
                lines = [flat[pl.ds(base + r * pitch, 4), :] + patches[pl.ds(s * ODD + r * 4, 4), :] for r in range(4)]
                for r in range(4):
                    flat[pl.ds(base + r * pitch, 4), :] = lines[r]
            return c

        lax.fori_loop(0, chunk_slots // UNROLL, spread, 0)
        return carry

    lax.fori_loop(0, col_ref.shape[1] // chunk_slots, chunk, 0)
    send = pltpu.make_async_copy(inner, grad_ref, sem)
    send.start()
    north_ref[...] = pad[0]
    south_ref[...] = pad[rows + 1]
    west_ref[...] = flat[pl.ds(pitch + EDGE - 1, rows, stride=pitch), :]
    east_ref[...] = flat[pl.ds(pitch + EDGE + cols, rows, stride=pitch), :]
    send.wait()


def neighbour(way):
    p = lax.axis_index("lat") + way[0]
    q = lax.axis_index("lon") + way[1]
    inside = (p >= 0) & (p < lax.axis_size("lat")) & (q >= 0) & (q < lax.axis_size("lon"))
    return (p, q), inside


def greet():
    barrier = pltpu.get_barrier_semaphore()
    for way in WAYS:
        device, inside = neighbour(way)

        @pl.when(inside)
        def _(device=device):
            pl.semaphore_signal(barrier, inc=1, device_id=device, device_id_type=pl.DeviceIdType.MESH)

    p, q = lax.axis_index("lat"), lax.axis_index("lon")
    near_lat = jnp.minimum(p + 1, lax.axis_size("lat") - 1) - jnp.maximum(p - 1, 0) + 1
    near_lon = jnp.minimum(q + 1, lax.axis_size("lon") - 1) - jnp.maximum(q - 1, 0) + 1
    pl.semaphore_wait(barrier, near_lat * near_lon - 1)


def exchange(moves, send_sems, recv_sems):
    def copy(i):
        way = WAYS[i]
        device, inside = neighbour(way)
        source, target = moves[way]
        return pltpu.make_async_remote_copy(
            src_ref=source, dst_ref=target, send_sem=send_sems.at[i], recv_sem=recv_sems.at[i],
            device_id=device, device_id_type=pl.DeviceIdType.MESH), inside

    for i in range(len(WAYS)):
        _, inside = neighbour(WAYS[i])

        @pl.when(inside)
        def _(i=i):
            copy(i)[0].start()

    for i in range(len(WAYS)):
        _, behind = neighbour((-WAYS[i][0], -WAYS[i][1]))

        @pl.when(jnp.logical_not(behind))
        def _(i=i):
            target = moves[WAYS[i]][1]
            target[...] = jnp.zeros(target.shape, F32)

    for i in range(len(WAYS)):
        _, inside = neighbour(WAYS[i])
        _, behind = neighbour((-WAYS[i][0], -WAYS[i][1]))

        @pl.when(inside)
        def _(i=i):
            copy(i)[0].wait_send()

        @pl.when(behind)
        def _(i=i):
            copy(i)[0].wait_recv()


def halo_kernel(control_ref, north_ref, south_ref, west_ref, east_ref, tiles, ends, sides, send_sems, recv_sems, sems):
    rows, cols, _ = control_ref.shape
    loads = [
        pltpu.make_async_copy(control_ref.at[:, pl.ds(0, 8), :], tiles.at[0], sems.at[0]),
        pltpu.make_async_copy(control_ref.at[:, pl.ds(cols - 8, 8), :], tiles.at[1], sems.at[1]),
        pltpu.make_async_copy(control_ref.at[0], ends.at[0], sems.at[2]),
        pltpu.make_async_copy(control_ref.at[rows - 1], ends.at[1], sems.at[3]),
    ]
    for load in loads:
        load.start()
    greet()
    for load in loads:
        load.wait()
    sides[0] = tiles[0, :, 0, :]
    sides[1] = tiles[1, :, 7, :]
    low, high = pl.ds(0, EDGE), pl.ds(rows + EDGE, EDGE)
    first, last = pl.ds(0, EDGE), pl.ds(rows - EDGE, EDGE)
    exchange({
        (1, 0): (ends.at[1], north_ref),
        (-1, 0): (ends.at[0], south_ref),
        (0, 1): (sides.at[1], west_ref.at[pl.ds(EDGE, rows), :]),
        (0, -1): (sides.at[0], east_ref.at[pl.ds(EDGE, rows), :]),
        (1, 1): (sides.at[1, last, :], west_ref.at[low, :]),
        (1, -1): (sides.at[0, last, :], east_ref.at[low, :]),
        (-1, 1): (sides.at[1, first, :], west_ref.at[high, :]),
        (-1, -1): (sides.at[0, first, :], east_ref.at[high, :]),
    }, send_sems, recv_sems)


def edges_kernel(out_n, out_s, out_w, out_e, got_n, got_s, got_w, got_e, nw, ne, sw, se, send_sems, recv_sems):
    cols = out_n.shape[0] - 2 * EDGE
    middle, low, high = pl.ds(EDGE, cols), pl.ds(0, EDGE), pl.ds(cols + EDGE, EDGE)
    greet()
    exchange({
        (1, 0): (out_s.at[middle, :], got_n),
        (-1, 0): (out_n.at[middle, :], got_s),
        (0, 1): (out_e, got_w),
        (0, -1): (out_w, got_e),
        (1, 1): (out_s.at[high, :], nw),
        (1, -1): (out_s.at[low, :], ne),
        (-1, 1): (out_n.at[high, :], sw),
        (-1, -1): (out_n.at[low, :], se),
    }, send_sems, recv_sems)


def finish_kernel(north_ref, south_ref, west_ref, east_ref, nw_ref, ne_ref, sw_ref, se_ref, grad_in,
                  grad_ref, line_n, line_s, tile_w, tile_e, sems):
    rows, cols, _ = grad_in.shape
    inner = pl.ds(1, rows - 2)
    ends = ((grad_ref.at[0], line_n), (grad_ref.at[rows - 1], line_s),
            (grad_ref.at[inner, pl.ds(0, 8), :], tile_w), (grad_ref.at[inner, pl.ds(cols - 8, 8), :], tile_e))
    loads = [pltpu.make_async_copy(far, near, sems.at[i]) for i, (far, near) in enumerate(ends)]
    for copy in loads:
        copy.start()
    for copy in loads:
        copy.wait()
    line_n[...] += north_ref[...]
    line_s[...] += south_ref[...]
    line_n[0:1, :] += west_ref[0:1, :] + nw_ref[0:1, :]
    line_n[cols - 1:cols, :] += east_ref[0:1, :] + ne_ref[7:8, :]
    line_s[0:1, :] += west_ref[rows - 1:rows, :] + sw_ref[0:1, :]
    line_s[cols - 1:cols, :] += east_ref[rows - 1:rows, :] + se_ref[7:8, :]

    flat_w = tile_w.reshape((rows - 2) * 8, 128)
    flat_e = tile_e.reshape((rows - 2) * 8, 128)
    flat_w[pl.ds(0, rows - 2, stride=8), :] += west_ref[1:rows - 1, :]
    flat_e[pl.ds(7, rows - 2, stride=8), :] += east_ref[1:rows - 1, :]
    stores = [pltpu.make_async_copy(near, far, sems.at[i]) for i, (far, near) in enumerate(ends)]
    for copy in stores:
        copy.start()
    for copy in stores:
        copy.wait()


def body(control, corr_blocks, jacobian, obs_values, obs_count, obs_col, obs_frac, obs_rinv):
    n_devices = lax.axis_size("lat") * lax.axis_size("lon")
    rows, cols, levels = control.shape
    channels = jacobian.shape[1]
    slots = obs_col.shape[1]
    pitch = cols + 2 * EDGE
    vmem = pl.BlockSpec(memory_space=pltpu.VMEM)
    smem = pl.BlockSpec(memory_space=pltpu.SMEM)
    hbm = pl.BlockSpec(memory_space=pl.ANY)

    incoming = lax.all_to_all(obs_values.reshape(n_devices, CAP, channels), ("lat", "lon"),
                              split_axis=0, concat_axis=0, tiled=True)
    def struct(count):
        return jax.ShapeDtypeStruct((count, levels), F32)

    north, south, west, east = pl.pallas_call(
        halo_kernel,
        out_shape=[struct(cols), struct(cols), struct(rows + 2 * EDGE), struct(rows + 2 * EDGE)],
        in_specs=[hbm],
        out_specs=[vmem] * 4,
        scratch_shapes=[
            pltpu.VMEM((2, rows, 8, levels), F32),
            pltpu.VMEM((2, cols, levels), F32),
            pltpu.VMEM((2, rows, levels), F32),
            pltpu.SemaphoreType.DMA((8,)),
            pltpu.SemaphoreType.DMA((8,)),
            pltpu.SemaphoreType.DMA((4,)),
        ],
        compiler_params=pltpu.CompilerParams(collective_id=0, has_side_effects=True, vmem_limit_bytes=56 * 2**20),
        name="halo",
    )(control)

    chunk_slots = math.gcd(slots, 512)
    limit = pltpu.CompilerParams(vmem_limit_bytes=56 * 2**20)
    evolved = pl.pallas_call(
        functools.partial(forward_kernel, pitch, chunk_slots),
        out_shape=jax.ShapeDtypeStruct((slots, channels), F32),
        in_specs=[smem] + [vmem] * 7 + [hbm],
        out_specs=vmem,
        scratch_shapes=[
            pltpu.VMEM((rows + 2, pitch, levels), F32),
            pltpu.VMEM((ODD * chunk_slots, levels), F32),
            pltpu.VMEM((2 * chunk_slots, 9 * levels), BF16),
            pltpu.VMEM((9 * levels, 2 * channels), BF16),
            pltpu.SemaphoreType.DMA,
        ],
        compiler_params=limit,
        cost_estimate=pl.CostEstimate(flops=2 * slots * 1152 * 512, bytes_accessed=40 * 2**20, transcendentals=0),
        name="forward",
    )(obs_col, obs_frac, corr_blocks, jacobian, north, south, west, east, control)

    departure = evolved - incoming.reshape(slots, channels).astype(F32)
    live = (jnp.arange(CAP, dtype=jnp.int32)[None, :] < obs_count[0][:, None]).reshape(slots, 1)
    weighted = jnp.where(live, obs_rinv[0][:, None] * departure, jnp.zeros_like(departure))
    returned = lax.all_to_all(weighted.astype(BF16).reshape(n_devices, CAP, channels), ("lat", "lon"),
                              split_axis=0, concat_axis=0, tiled=True)

    gradient, out_n, out_s, out_w, out_e = pl.pallas_call(
        functools.partial(adjoint_kernel, pitch, chunk_slots),
        out_shape=[
            jax.ShapeDtypeStruct(control.shape, F32),
            jax.ShapeDtypeStruct((pitch, levels), F32),
            jax.ShapeDtypeStruct((pitch, levels), F32),
            jax.ShapeDtypeStruct((rows, levels), F32),
            jax.ShapeDtypeStruct((rows, levels), F32),
        ],
        in_specs=[smem] + [vmem] * 4 + [hbm],
        out_specs=[hbm] + [vmem] * 4,
        scratch_shapes=[
            pltpu.VMEM((rows + 2, pitch, levels), F32),
            pltpu.VMEM((ODD * chunk_slots, levels), F32),
            pltpu.VMEM((chunk_slots, 9 * levels), F32),
            pltpu.VMEM((2 * channels, 9 * levels), BF16),
            pltpu.VMEM((2 * channels, 9 * levels), BF16),
            pltpu.SemaphoreType.DMA,
        ],
        compiler_params=limit,
        cost_estimate=pl.CostEstimate(flops=2 * slots * 1152 * 512, bytes_accessed=60 * 2**20, transcendentals=0),
        name="adjoint",
    )(obs_col, obs_frac, corr_blocks, jacobian, weighted, control)

    got = pl.pallas_call(
        edges_kernel,
        out_shape=[struct(cols), struct(cols), struct(rows), struct(rows)] + [struct(EDGE)] * 4,
        in_specs=[vmem] * 4,
        out_specs=[vmem] * 8,
        scratch_shapes=[pltpu.SemaphoreType.DMA((8,)), pltpu.SemaphoreType.DMA((8,))],
        compiler_params=pltpu.CompilerParams(collective_id=1, has_side_effects=True),
        name="edges",
    )(out_n, out_s, out_w, out_e)
    gradient = pl.pallas_call(
        finish_kernel,
        out_shape=jax.ShapeDtypeStruct(control.shape, F32),
        in_specs=[vmem] * 8 + [hbm],
        out_specs=hbm,
        scratch_shapes=[
            pltpu.VMEM((cols, levels), F32),
            pltpu.VMEM((cols, levels), F32),
            pltpu.VMEM((rows - 2, 8, levels), F32),
            pltpu.VMEM((rows - 2, 8, levels), F32),
            pltpu.SemaphoreType.DMA((4,)),
        ],
        input_output_aliases={8: 0},
        name="finish",
    )(*got, gradient)
    return (gradient, returned.reshape(n_devices * CAP, channels))


def solution(mesh):
    in_specs = (
        P("lat", "lon", None),
        P(),
        P(),
        P(("lat", "lon"), None),
        P(("lat", "lon"), None),
        P(("lat", "lon"), None),
        P(("lat", "lon"), None, None),
        P(("lat", "lon"), None),
    )
    out_specs = (P("lat", "lon", None), P(("lat", "lon"), None))
    return jax.shard_map(body, mesh=mesh, in_specs=in_specs, out_specs=out_specs, check_vma=False)
```

```python
import functools
import math
import jax
import jax.numpy as jnp
from jax import lax
from jax.experimental import pallas as pl
from jax.experimental.pallas import tpu as pltpu
from jax.sharding import PartitionSpec as P

CAP = 64
SUB = 128
ODD = 17
EDGE = 8
F32 = jnp.float32
BF16 = jnp.bfloat16
UNROLL = 8
WAYS = ((1, 0), (-1, 0), (0, 1), (0, -1), (1, 1), (1, -1), (-1, 1), (-1, -1))


def split(x):
    hi = x.astype(BF16)
    return hi, (x - hi.astype(F32)).astype(BF16)


def column(row):
    return jnp.broadcast_to(row, (128, SUB)).T


def combined(corr_ref, jac_ref, k):
    return jnp.dot(corr_ref[k], jac_ref[...], precision=lax.Precision.HIGHEST, preferred_element_type=F32)


def place(corner, cols, pitch):
    if cols & (cols - 1) == 0:
        line = lax.shift_right_logical(corner, cols.bit_length() - 1)
    else:
        line = lax.div(corner, cols)
    return corner + line * (pitch - cols) + (EDGE - 1)


def forward_kernel(pitch, chunk_slots, col_ref, count_ref, frac_ref, rinv_ref, observed_ref, g_both,
                   north_ref, south_ref, west_ref, east_ref, control_ref, weighted_ref, rounded_ref,
                   pad, patches, p_both, sem):
    rows, cols, _ = control_ref.shape
    fetch = pltpu.make_async_copy(control_ref, pad.at[pl.ds(1, rows), pl.ds(EDGE, cols), :], sem)
    fetch.start()
    flat = pad.reshape((rows + 2) * pitch, 128)
    pad[0, EDGE:EDGE + cols, :] = north_ref[...]
    pad[rows + 1, EDGE:EDGE + cols, :] = south_ref[...]
    flat[pl.ds(EDGE - 1, rows + 2, stride=pitch), :] = west_ref[EDGE - 1:EDGE + rows + 1, :]
    flat[pl.ds(EDGE + cols, rows + 2, stride=pitch), :] = east_ref[EDGE - 1:EDGE + rows + 1, :]
    fetch.wait()

    def chunk(n, carry):
        first = n * chunk_slots

        def pick(t, c):
            lines = []
            for v in range(UNROLL):
                base = place(col_ref[0, first + t * UNROLL + v], cols, pitch)
                lines.append([flat[pl.ds(base + r * pitch, 4), :] for r in range(4)])
            for v in range(UNROLL):
                for r in range(4):
                    patches[pl.ds((t * UNROLL + v) * ODD + r * 4, 4), :] = lines[v][r]
            return c

        lax.fori_loop(0, chunk_slots // UNROLL, pick, 0)

        def mix(m, c):
            at = pl.ds(pl.multiple_of(first + m * SUB, SUB), SUB)
            hi_at = pl.ds(pl.multiple_of(m * SUB, SUB), SUB)
            lo_at = pl.ds(pl.multiple_of(chunk_slots + m * SUB, SUB), SUB)
            f = column(frac_ref[0, 0:1, at])
            g = column(frac_ref[0, 1:2, at])
            origin = m * (SUB * ODD)
            for a in range(3):
                lat = []
                for q in range(4):
                    low = patches[pl.ds(origin + a * 4 + q, SUB, stride=ODD), :]
                    high = patches[pl.ds(origin + a * 4 + 4 + q, SUB, stride=ODD), :]
                    lat.append((1.0 - f) * low + f * high)
                for b in range(3):
                    hi, lo = split((1.0 - g) * lat[b] + g * lat[b + 1])
                    k = 3 * a + b
                    p_both[hi_at, k * 128:(k + 1) * 128] = hi
                    p_both[lo_at, k * 128:(k + 1) * 128] = lo
            return c

        lax.fori_loop(0, chunk_slots // SUB, mix, 0)
        both = jnp.dot(p_both[...], g_both[...], preferred_element_type=F32)
        for m in range(chunk_slots // SUB):
            hi, lo = both[m * SUB:(m + 1) * SUB], both[chunk_slots + m * SUB:chunk_slots + (m + 1) * SUB]
            evolved = hi[:, 0:128] + (hi[:, 128:256] + lo[:, 0:128] + lo[:, 128:256])
            start = pl.multiple_of(first + m * SUB, SUB)
            at = pl.ds(start, SUB)
            lane = lax.broadcasted_iota(jnp.int32, (1, SUB), 1)
            live = jnp.zeros((1, SUB), jnp.int32)
            for part in range(SUB // CAP):
                count = count_ref[0, n * (chunk_slots // CAP) + m * (SUB // CAP) + part]
                live += ((lane >= part * CAP) & (lane < part * CAP + count)).astype(jnp.int32)
            rinv = jnp.where(live > 0, rinv_ref[0:1, at], 0.0)
            weighted = column(rinv) * (evolved - observed_ref[at, :].astype(F32))
            weighted_ref[at, :] = weighted
            rounded_ref[at, :] = weighted.astype(BF16)
        return carry

    lax.fori_loop(0, col_ref.shape[1] // chunk_slots, chunk, 0)


def adjoint_kernel(pitch, chunk_slots, col_ref, frac_ref, gt_hi, gt_lo, weighted_ref, control_ref,
                   grad_ref, north_ref, south_ref, west_ref, east_ref, pad, patches, q_ref, sem):
    rows, cols, _ = control_ref.shape
    inner = pad.at[pl.ds(1, rows), pl.ds(EDGE, cols), :]
    fetch = pltpu.make_async_copy(control_ref, inner, sem)
    fetch.start()
    for i in (0, rows + 1):
        pad[i] = jnp.zeros((pitch, 128), F32)

    def clear(i, c):
        pad[pl.ds(i, 1), 0:EDGE, :] = jnp.zeros((1, EDGE, 128), F32)
        pad[pl.ds(i, 1), EDGE + cols:pitch, :] = jnp.zeros((1, pitch - cols - EDGE, 128), F32)
        return c

    lax.fori_loop(1, rows + 1, clear, 0)
    fetch.wait()
    flat = pad.reshape((rows + 2) * pitch, 128)

    def chunk(n, carry):
        first = n * chunk_slots
        w_hi, w_lo = split(weighted_ref[pl.ds(pl.multiple_of(first, chunk_slots), chunk_slots), :])
        w = jnp.concatenate([w_hi, w_lo], axis=1)
        q_ref[...] = (jnp.dot(w, gt_hi[...], preferred_element_type=F32)
                      + jnp.dot(w, gt_lo[...], preferred_element_type=F32))

        def mix(m, carry):
            at = pl.ds(pl.multiple_of(first + m * SUB, SUB), SUB)
            here = pl.ds(pl.multiple_of(m * SUB, SUB), SUB)
            f = column(frac_ref[0, 0:1, at])
            g = column(frac_ref[0, 1:2, at])
            origin = m * (SUB * ODD)
            for c in range(4):
                line = []
                for a in range(3):
                    part = None
                    if c < 3:
                        part = (1.0 - g) * q_ref[here, (3 * a + c) * 128:(3 * a + c + 1) * 128]
                    if c > 0:
                        other = g * q_ref[here, (3 * a + c - 1) * 128:(3 * a + c) * 128]
                        part = other if part is None else part + other
                    line.append(part)
                for r in range(4):
                    part = None
                    if r < 3:
                        part = (1.0 - f) * line[r]
                    if r > 0:
                        other = f * line[r - 1]
                        part = other if part is None else part + other
                    patches[pl.ds(origin + r * 4 + c, SUB, stride=ODD), :] = part
            return carry

        lax.fori_loop(0, chunk_slots // SUB, mix, 0)

        def spread(t, c):
            bases, terms = [], []
            for v in range(UNROLL):
                s = t * UNROLL + v
                bases.append(place(col_ref[0, first + s], cols, pitch))
                terms.append([patches[pl.ds(s * ODD + r * 4, 4), :] for r in range(4)])
            for v in range(UNROLL):
                lines = [flat[pl.ds(bases[v] + r * pitch, 4), :] + terms[v][r] for r in range(4)]
                for r in range(4):
                    flat[pl.ds(bases[v] + r * pitch, 4), :] = lines[r]
            return c

        lax.fori_loop(0, chunk_slots // UNROLL, spread, 0)
        return carry

    lax.fori_loop(0, col_ref.shape[1] // chunk_slots, chunk, 0)
    send = pltpu.make_async_copy(inner, grad_ref, sem)
    send.start()
    north_ref[...] = pad[0]
    south_ref[...] = pad[rows + 1]
    west_ref[...] = flat[pl.ds(pitch + EDGE - 1, rows, stride=pitch), :]
    east_ref[...] = flat[pl.ds(pitch + EDGE + cols, rows, stride=pitch), :]
    send.wait()


def neighbour(way):
    p = lax.axis_index("lat") + way[0]
    q = lax.axis_index("lon") + way[1]
    inside = (p >= 0) & (p < lax.axis_size("lat")) & (q >= 0) & (q < lax.axis_size("lon"))
    return (p, q), inside


def everyone():
    n_lon = lax.axis_size("lon")
    count = lax.axis_size("lat") * n_lon
    return lax.axis_index("lat") * n_lon + lax.axis_index("lon"), count, n_lon


def greet():
    me, count, n_lon = everyone()
    barrier = pltpu.get_barrier_semaphore()

    def signal(k, c):
        peer = lax.rem(me + k, count)
        pl.semaphore_signal(barrier, inc=1, device_id=(lax.div(peer, n_lon), lax.rem(peer, n_lon)),
                            device_id_type=pl.DeviceIdType.MESH)
        return c

    lax.fori_loop(1, count, signal, 0)
    pl.semaphore_wait(barrier, count - 1)


def swap_blocks(source, target, send_sems, recv_sems, own_sem):
    me, count, n_lon = everyone()

    def block(ref, d):
        return ref.at[pl.ds(pl.multiple_of(d * CAP, CAP), CAP), :]

    def copy(k):
        peer = lax.rem(me + k, count)
        return pltpu.make_async_remote_copy(
            src_ref=block(source, peer), dst_ref=block(target, me), send_sem=send_sems.at[k], recv_sem=recv_sems.at[k],
            device_id=(lax.div(peer, n_lon), lax.rem(peer, n_lon)), device_id_type=pl.DeviceIdType.MESH)

    own = pltpu.make_async_copy(block(source, me), block(target, me), own_sem)

    def start():
        own.start()

        def one(k, c):
            copy(k).start()
            return c

        lax.fori_loop(1, count, one, 0)

    def wait():
        def one(k, c):
            copy(k).wait_send()
            came = lax.rem(me - k + count, count)
            pltpu.make_async_remote_copy(
                src_ref=block(source, came), dst_ref=block(target, came), send_sem=send_sems.at[k],
                recv_sem=recv_sems.at[k], device_id=(lax.div(came, n_lon), lax.rem(came, n_lon)),
                device_id_type=pl.DeviceIdType.MESH).wait_recv()
            return c

        lax.fori_loop(1, count, one, 0)
        own.wait()

    return start, wait


def exchange(moves, send_sems, recv_sems):
    def copy(i):
        way = WAYS[i]
        device, inside = neighbour(way)
        source, target = moves[way]
        return pltpu.make_async_remote_copy(
            src_ref=source, dst_ref=target, send_sem=send_sems.at[i], recv_sem=recv_sems.at[i],
            device_id=device, device_id_type=pl.DeviceIdType.MESH), inside

    def start():
        for i in range(len(WAYS)):
            _, inside = neighbour(WAYS[i])

            @pl.when(inside)
            def _(i=i):
                copy(i)[0].start()

    def wait():
        for i in range(len(WAYS)):
            _, behind = neighbour((-WAYS[i][0], -WAYS[i][1]))

            @pl.when(jnp.logical_not(behind))
            def _(i=i):
                target = moves[WAYS[i]][1]
                target[...] = jnp.zeros(target.shape, F32)

        for i in range(len(WAYS)):
            _, inside = neighbour(WAYS[i])
            _, behind = neighbour((-WAYS[i][0], -WAYS[i][1]))

            @pl.when(inside)
            def _(i=i):
                copy(i)[0].wait_send()

            @pl.when(behind)
            def _(i=i):
                copy(i)[0].wait_recv()

    return start, wait


def front_kernel(control_ref, values_ref, corr_ref, jac_ref,
                 north_ref, south_ref, west_ref, east_ref, observed_ref, g_both, gt_hi, gt_lo,
                 tiles, ends, sides, send_sems, recv_sems, sems, far_send, far_recv):
    rows, cols, _ = control_ref.shape
    loads = [
        pltpu.make_async_copy(control_ref.at[:, pl.ds(0, 8), :], tiles.at[0], sems.at[0]),
        pltpu.make_async_copy(control_ref.at[:, pl.ds(cols - 8, 8), :], tiles.at[1], sems.at[1]),
        pltpu.make_async_copy(control_ref.at[0], ends.at[0], sems.at[2]),
        pltpu.make_async_copy(control_ref.at[rows - 1], ends.at[1], sems.at[3]),
    ]
    for load in loads:
        load.start()
    greet()
    for load in loads:
        load.wait()
    sides[0] = tiles[0, :, 0, :]
    sides[1] = tiles[1, :, 7, :]
    low, high = pl.ds(0, EDGE), pl.ds(rows + EDGE, EDGE)
    first, last = pl.ds(0, EDGE), pl.ds(rows - EDGE, EDGE)
    start_halo, wait_halo = exchange({
        (1, 0): (ends.at[1], north_ref),
        (-1, 0): (ends.at[0], south_ref),
        (0, 1): (sides.at[1], west_ref.at[pl.ds(EDGE, rows), :]),
        (0, -1): (sides.at[0], east_ref.at[pl.ds(EDGE, rows), :]),
        (1, 1): (sides.at[1, last, :], west_ref.at[low, :]),
        (1, -1): (sides.at[0, last, :], east_ref.at[low, :]),
        (-1, 1): (sides.at[1, first, :], west_ref.at[high, :]),
        (-1, -1): (sides.at[0, first, :], east_ref.at[high, :]),
    }, send_sems, recv_sems)
    start_blocks, wait_blocks = swap_blocks(values_ref, observed_ref, far_send, far_recv, sems.at[4])
    start_halo()
    start_blocks()
    for k in range(9):
        g = combined(corr_ref, jac_ref, k)
        hi, lo = split(g)
        g_both[k * 128:(k + 1) * 128, 0:128] = hi
        g_both[k * 128:(k + 1) * 128, 128:256] = lo
        hi, lo = split(g.T)
        for half in range(2):
            gt_hi[half * 128:(half + 1) * 128, k * 128:(k + 1) * 128] = hi
            gt_lo[half * 128:(half + 1) * 128, k * 128:(k + 1) * 128] = lo
    wait_halo()
    wait_blocks()


def back_kernel(out_n, out_s, out_w, out_e, rounded_ref, got_n, got_s, got_w, got_e, nw, ne, sw, se, returned_ref,
                send_sems, recv_sems, far_send, far_recv, own_sem):
    cols = out_n.shape[0] - 2 * EDGE
    middle, low, high = pl.ds(EDGE, cols), pl.ds(0, EDGE), pl.ds(cols + EDGE, EDGE)
    greet()
    start_edges, wait_edges = exchange({
        (1, 0): (out_s.at[middle, :], got_n),
        (-1, 0): (out_n.at[middle, :], got_s),
        (0, 1): (out_e, got_w),
        (0, -1): (out_w, got_e),
        (1, 1): (out_s.at[high, :], nw),
        (1, -1): (out_s.at[low, :], ne),
        (-1, 1): (out_n.at[high, :], sw),
        (-1, -1): (out_n.at[low, :], se),
    }, send_sems, recv_sems)
    start_blocks, wait_blocks = swap_blocks(rounded_ref, returned_ref, far_send, far_recv, own_sem)
    start_edges()
    start_blocks()
    wait_edges()
    wait_blocks()


def finish_kernel(north_ref, south_ref, west_ref, east_ref, nw_ref, ne_ref, sw_ref, se_ref, grad_in,
                  grad_ref, line_n, line_s, tile_w, tile_e, sems):
    rows, cols, _ = grad_in.shape
    inner = pl.ds(1, rows - 2)
    ends = ((grad_ref.at[0], line_n), (grad_ref.at[rows - 1], line_s),
            (grad_ref.at[inner, pl.ds(0, 8), :], tile_w), (grad_ref.at[inner, pl.ds(cols - 8, 8), :], tile_e))
    loads = [pltpu.make_async_copy(far, near, sems.at[i]) for i, (far, near) in enumerate(ends)]
    for copy in loads:
        copy.start()
    for copy in loads:
        copy.wait()
    line_n[...] += north_ref[...]
    line_s[...] += south_ref[...]
    line_n[0:1, :] += west_ref[0:1, :] + nw_ref[0:1, :]
    line_n[cols - 1:cols, :] += east_ref[0:1, :] + ne_ref[7:8, :]
    line_s[0:1, :] += west_ref[rows - 1:rows, :] + sw_ref[0:1, :]
    line_s[cols - 1:cols, :] += east_ref[rows - 1:rows, :] + se_ref[7:8, :]

    flat_w = tile_w.reshape((rows - 2) * 8, 128)
    flat_e = tile_e.reshape((rows - 2) * 8, 128)
    flat_w[pl.ds(0, rows - 2, stride=8), :] += west_ref[1:rows - 1, :]
    flat_e[pl.ds(7, rows - 2, stride=8), :] += east_ref[1:rows - 1, :]
    stores = [pltpu.make_async_copy(near, far, sems.at[i]) for i, (far, near) in enumerate(ends)]
    for copy in stores:
        copy.start()
    for copy in stores:
        copy.wait()


def body(control, corr_blocks, jacobian, obs_values, obs_count, obs_col, obs_frac, obs_rinv):
    n_devices = lax.axis_size("lat") * lax.axis_size("lon")
    rows, cols, levels = control.shape
    channels = jacobian.shape[1]
    slots = obs_col.shape[1]
    pitch = cols + 2 * EDGE
    vmem = pl.BlockSpec(memory_space=pltpu.VMEM)
    smem = pl.BlockSpec(memory_space=pltpu.SMEM)
    hbm = pl.BlockSpec(memory_space=pl.ANY)

    def struct(count):
        return jax.ShapeDtypeStruct((count, levels), F32)

    north, south, west, east, observed, g_both, gt_hi, gt_lo = pl.pallas_call(
        front_kernel,
        out_shape=[struct(cols), struct(cols), struct(rows + 2 * EDGE), struct(rows + 2 * EDGE),
                   jax.ShapeDtypeStruct((slots, channels), BF16),
                   jax.ShapeDtypeStruct((9 * levels, 2 * channels), BF16),
                   jax.ShapeDtypeStruct((2 * channels, 9 * levels), BF16),
                   jax.ShapeDtypeStruct((2 * channels, 9 * levels), BF16)],
        in_specs=[hbm, hbm, vmem, vmem],
        out_specs=[vmem] * 8,
        scratch_shapes=[
            pltpu.VMEM((2, rows, 8, levels), F32),
            pltpu.VMEM((2, cols, levels), F32),
            pltpu.VMEM((2, rows, levels), F32),
            pltpu.SemaphoreType.DMA((8,)),
            pltpu.SemaphoreType.DMA((8,)),
            pltpu.SemaphoreType.DMA((5,)),
            pltpu.SemaphoreType.DMA((n_devices,)),
            pltpu.SemaphoreType.DMA((n_devices,)),
        ],
        compiler_params=pltpu.CompilerParams(collective_id=0, has_side_effects=True, vmem_limit_bytes=56 * 2**20),
        name="front",
    )(control, obs_values, corr_blocks, jacobian)

    chunk_slots = math.gcd(slots, 512)
    limit = pltpu.CompilerParams(vmem_limit_bytes=56 * 2**20)
    weighted, rounded = pl.pallas_call(
        functools.partial(forward_kernel, pitch, chunk_slots),
        out_shape=[jax.ShapeDtypeStruct((slots, channels), F32), jax.ShapeDtypeStruct((slots, channels), BF16)],
        in_specs=[smem, smem] + [vmem] * 8 + [hbm],
        out_specs=[vmem, vmem],
        scratch_shapes=[
            pltpu.VMEM((rows + 2, pitch, levels), F32),
            pltpu.VMEM((ODD * chunk_slots, levels), F32),
            pltpu.VMEM((2 * chunk_slots, 9 * levels), BF16),
            pltpu.SemaphoreType.DMA,
        ],
        compiler_params=limit,
        cost_estimate=pl.CostEstimate(flops=2 * slots * 1152 * 512, bytes_accessed=40 * 2**20, transcendentals=0),
        name="forward",
    )(obs_col, obs_count, obs_frac, obs_rinv, observed, g_both, north, south, west, east, control)

    gradient, out_n, out_s, out_w, out_e = pl.pallas_call(
        functools.partial(adjoint_kernel, pitch, chunk_slots),
        out_shape=[
            jax.ShapeDtypeStruct(control.shape, F32),
            jax.ShapeDtypeStruct((pitch, levels), F32),
            jax.ShapeDtypeStruct((pitch, levels), F32),
            jax.ShapeDtypeStruct((rows, levels), F32),
            jax.ShapeDtypeStruct((rows, levels), F32),
        ],
        in_specs=[smem] + [vmem] * 4 + [hbm],
        out_specs=[hbm] + [vmem] * 4,
        scratch_shapes=[
            pltpu.VMEM((rows + 2, pitch, levels), F32),
            pltpu.VMEM((ODD * chunk_slots, levels), F32),
            pltpu.VMEM((chunk_slots, 9 * levels), F32),
            pltpu.SemaphoreType.DMA,
        ],
        compiler_params=limit,
        cost_estimate=pl.CostEstimate(flops=2 * slots * 1152 * 512, bytes_accessed=60 * 2**20, transcendentals=0),
        name="adjoint",
    )(obs_col, obs_frac, gt_hi, gt_lo, weighted, control)

    *got, returned = pl.pallas_call(
        back_kernel,
        out_shape=[struct(cols), struct(cols), struct(rows), struct(rows)] + [struct(EDGE)] * 4
        + [jax.ShapeDtypeStruct((slots, channels), BF16)],
        in_specs=[vmem] * 4 + [hbm],
        out_specs=[vmem] * 9,
        scratch_shapes=[
            pltpu.SemaphoreType.DMA((8,)),
            pltpu.SemaphoreType.DMA((8,)),
            pltpu.SemaphoreType.DMA((n_devices,)),
            pltpu.SemaphoreType.DMA((n_devices,)),
            pltpu.SemaphoreType.DMA,
        ],
        compiler_params=pltpu.CompilerParams(collective_id=1, has_side_effects=True),
        name="back",
    )(out_n, out_s, out_w, out_e, rounded)
    gradient = pl.pallas_call(
        finish_kernel,
        out_shape=jax.ShapeDtypeStruct(control.shape, F32),
        in_specs=[vmem] * 8 + [hbm],
        out_specs=hbm,
        scratch_shapes=[
            pltpu.VMEM((cols, levels), F32),
            pltpu.VMEM((cols, levels), F32),
            pltpu.VMEM((rows - 2, 8, levels), F32),
            pltpu.VMEM((rows - 2, 8, levels), F32),
            pltpu.SemaphoreType.DMA((4,)),
        ],
        input_output_aliases={8: 0},
        name="finish",
    )(*got, gradient)
    return (gradient, returned)


def solution(mesh):
    in_specs = (
        P("lat", "lon", None),
        P(),
        P(),
        P(("lat", "lon"), None),
        P(("lat", "lon"), None),
        P(("lat", "lon"), None),
        P(("lat", "lon"), None, None),
        P(("lat", "lon"), None),
    )
    out_specs = (P("lat", "lon", None), P(("lat", "lon"), None))
    return jax.shard_map(body, mesh=mesh, in_specs=in_specs, out_specs=out_specs, check_vma=False)
```

```python
import functools
import math
import jax
import jax.numpy as jnp
from jax import lax
from jax.experimental import pallas as pl
from jax.experimental.pallas import tpu as pltpu
from jax.sharding import PartitionSpec as P

CAP = 64
SUB = 128
ODD = 17
EDGE = 8
F32 = jnp.float32
BF16 = jnp.bfloat16
WAYS = ((1, 0), (-1, 0), (0, 1), (0, -1), (1, 1), (1, -1), (-1, 1), (-1, -1))


def split(x):
    hi = x.astype(BF16)
    return hi, (x - hi.astype(F32)).astype(BF16)


def column(row):
    return jnp.broadcast_to(row, (128, SUB)).T


def combined(corr_ref, jac_ref, k):
    return jnp.dot(corr_ref[k], jac_ref[...], precision=lax.Precision.HIGHEST, preferred_element_type=F32)


def place(corner, cols, pitch):
    if cols & (cols - 1) == 0:
        line = lax.shift_right_logical(corner, cols.bit_length() - 1)
    else:
        line = lax.div(corner, cols)
    return corner + line * (pitch - cols) + (EDGE - 1)


def forward_kernel(pitch, chunk_slots, col_ref, count_ref, frac_ref, rinv_ref, observed_ref, g_both,
                   north_ref, south_ref, west_ref, east_ref, control_ref, weighted_ref, rounded_ref,
                   pad, patches_a, patches_b, f_ref, g_ref, p_both, sem):
    rows, cols, _ = control_ref.shape
    fetch = pltpu.make_async_copy(control_ref, pad.at[pl.ds(1, rows), pl.ds(EDGE, cols), :], sem)
    fetch.start()
    flat = pad.reshape((rows + 2) * pitch, 128)
    pad[0, EDGE:EDGE + cols, :] = north_ref[...]
    pad[rows + 1, EDGE:EDGE + cols, :] = south_ref[...]
    flat[pl.ds(EDGE - 1, rows + 2, stride=pitch), :] = west_ref[EDGE - 1:EDGE + rows + 1, :]
    flat[pl.ds(EDGE + cols, rows + 2, stride=pitch), :] = east_ref[EDGE - 1:EDGE + rows + 1, :]
    fetch.wait()

    def chunk(n, carry):
        first = n * chunk_slots

        for m in range(chunk_slots // SUB):
            at = pl.ds(pl.multiple_of(first + m * SUB, SUB), SUB)
            f_ref[m * SUB:(m + 1) * SUB, :] = column(frac_ref[0, 0:1, at])
            g_ref[m * SUB:(m + 1) * SUB, :] = column(frac_ref[0, 1:2, at])

        def pick(start, patches):
            for v in range(8):
                base = place(col_ref[0, first + start + v], cols, pitch)
                for r in range(4):
                    patches[v * ODD + r * 4:v * ODD + r * 4 + 4, :] = flat[pl.ds(base + r * pitch, 4), :]

        def mix(start, patches):
            at = pl.ds(pl.multiple_of(start, 8), 8)
            f, g = f_ref[at, :], g_ref[at, :]
            lines = [[patches[pl.ds(r * 4 + q, 8, stride=ODD), :] for q in range(4)] for r in range(4)]
            mixed = []
            for a in range(3):
                lat = [(1.0 - f) * lines[a][q] + f * lines[a + 1][q] for q in range(4)]
                mixed.extend((1.0 - g) * lat[b] + g * lat[b + 1] for b in range(3))
            return mixed

        def pair(t, c):
            start = t * 16
            upper = mix(start, patches_a)
            pick(start + 8, patches_b)
            lower = mix(start + 8, patches_b)
            pick(jnp.minimum(start + 16, chunk_slots - 8), patches_a)
            hi_at = pl.ds(pl.multiple_of(start, 16), 16)
            lo_at = pl.ds(pl.multiple_of(chunk_slots + start, 16), 16)
            for k in range(9):
                hi, lo = split(jnp.concatenate([upper[k], lower[k]], axis=0))
                p_both[hi_at, k * 128:(k + 1) * 128] = hi
                p_both[lo_at, k * 128:(k + 1) * 128] = lo
            return c

        pick(0, patches_a)
        lax.fori_loop(0, chunk_slots // 16, pair, 0, unroll=2)
        both = jnp.dot(p_both[...], g_both[...], preferred_element_type=F32)
        for m in range(chunk_slots // SUB):
            hi, lo = both[m * SUB:(m + 1) * SUB], both[chunk_slots + m * SUB:chunk_slots + (m + 1) * SUB]
            evolved = hi[:, 0:128] + (hi[:, 128:256] + lo[:, 0:128] + lo[:, 128:256])
            start = pl.multiple_of(first + m * SUB, SUB)
            at = pl.ds(start, SUB)
            lane = lax.broadcasted_iota(jnp.int32, (1, SUB), 1)
            live = jnp.zeros((1, SUB), jnp.int32)
            for part in range(SUB // CAP):
                count = count_ref[0, n * (chunk_slots // CAP) + m * (SUB // CAP) + part]
                live += ((lane >= part * CAP) & (lane < part * CAP + count)).astype(jnp.int32)
            rinv = jnp.where(live > 0, rinv_ref[0:1, at], 0.0)
            weighted = column(rinv) * (evolved - observed_ref[at, :].astype(F32))
            weighted_ref[at, :] = weighted
            rounded_ref[at, :] = weighted.astype(BF16)
        return carry

    lax.fori_loop(0, col_ref.shape[1] // chunk_slots, chunk, 0)


def adjoint_kernel(pitch, chunk_slots, col_ref, frac_ref, gt_hi, gt_lo, weighted_ref, control_ref,
                   grad_ref, north_ref, south_ref, west_ref, east_ref, pad, patches_a, patches_b, f_ref, g_ref, q_ref, sem):
    rows, cols, _ = control_ref.shape
    inner = pad.at[pl.ds(1, rows), pl.ds(EDGE, cols), :]
    fetch = pltpu.make_async_copy(control_ref, inner, sem)
    fetch.start()
    for i in (0, rows + 1):
        pad[i] = jnp.zeros((pitch, 128), F32)

    def clear(i, c):
        pad[pl.ds(i, 1), 0:EDGE, :] = jnp.zeros((1, EDGE, 128), F32)
        pad[pl.ds(i, 1), EDGE + cols:pitch, :] = jnp.zeros((1, pitch - cols - EDGE, 128), F32)
        return c

    lax.fori_loop(1, rows + 1, clear, 0)
    fetch.wait()
    flat = pad.reshape((rows + 2) * pitch, 128)

    def chunk(n, carry):
        first = n * chunk_slots
        w_hi, w_lo = split(weighted_ref[pl.ds(pl.multiple_of(first, chunk_slots), chunk_slots), :])
        w = jnp.concatenate([w_hi, w_lo], axis=1)
        q_ref[...] = (jnp.dot(w, gt_hi[...], preferred_element_type=F32)
                      + jnp.dot(w, gt_lo[...], preferred_element_type=F32))

        for m in range(chunk_slots // SUB):
            at = pl.ds(pl.multiple_of(first + m * SUB, SUB), SUB)
            f_ref[m * SUB:(m + 1) * SUB, :] = column(frac_ref[0, 0:1, at])
            g_ref[m * SUB:(m + 1) * SUB, :] = column(frac_ref[0, 1:2, at])

        def mix(start, patches):
            at = pl.ds(pl.multiple_of(start, 8), 8)
            f, g = f_ref[at, :], g_ref[at, :]
            rest_f, rest_g = 1.0 - f, 1.0 - g
            q = [[q_ref[at, (3 * a + b) * 128:(3 * a + b + 1) * 128] for b in range(3)] for a in range(3)]
            for c in range(4):
                line = []
                for a in range(3):
                    terms = ([rest_g * q[a][c]] if c < 3 else []) + ([g * q[a][c - 1]] if c > 0 else [])
                    line.append(sum(terms[1:], terms[0]))
                for r in range(4):
                    terms = ([rest_f * line[r]] if r < 3 else []) + ([f * line[r - 1]] if r > 0 else [])
                    patches[pl.ds(r * 4 + c, 8, stride=ODD), :] = sum(terms[1:], terms[0])

        def spread(start, patches):
            for v in range(8):
                base = place(col_ref[0, first + start + v], cols, pitch)
                lines = [flat[pl.ds(base + r * pitch, 4), :] + patches[v * ODD + r * 4:v * ODD + r * 4 + 4, :]
                         for r in range(4)]
                for r in range(4):
                    flat[pl.ds(base + r * pitch, 4), :] = lines[r]

        def pair(t, c):
            start = t * 16
            mix(start + 8, patches_b)
            spread(start, patches_a)
            mix(jnp.minimum(start + 16, chunk_slots - 8), patches_a)
            spread(start + 8, patches_b)
            return c

        mix(0, patches_a)
        lax.fori_loop(0, chunk_slots // 16, pair, 0, unroll=2)
        return carry

    lax.fori_loop(0, col_ref.shape[1] // chunk_slots, chunk, 0)
    send = pltpu.make_async_copy(inner, grad_ref, sem)
    send.start()
    north_ref[...] = pad[0]
    south_ref[...] = pad[rows + 1]
    west_ref[...] = flat[pl.ds(pitch + EDGE - 1, rows, stride=pitch), :]
    east_ref[...] = flat[pl.ds(pitch + EDGE + cols, rows, stride=pitch), :]
    send.wait()


def neighbour(way):
    p = lax.axis_index("lat") + way[0]
    q = lax.axis_index("lon") + way[1]
    inside = (p >= 0) & (p < lax.axis_size("lat")) & (q >= 0) & (q < lax.axis_size("lon"))
    return (p, q), inside


def greet():
    barrier = pltpu.get_barrier_semaphore()
    for way in WAYS:
        device, inside = neighbour(way)

        @pl.when(inside)
        def _(device=device):
            pl.semaphore_signal(barrier, inc=1, device_id=device, device_id_type=pl.DeviceIdType.MESH)

    p, q = lax.axis_index("lat"), lax.axis_index("lon")
    near_lat = jnp.minimum(p + 1, lax.axis_size("lat") - 1) - jnp.maximum(p - 1, 0) + 1
    near_lon = jnp.minimum(q + 1, lax.axis_size("lon") - 1) - jnp.maximum(q - 1, 0) + 1
    pl.semaphore_wait(barrier, near_lat * near_lon - 1)


def exchange(moves, send_sems, recv_sems):
    def copy(i):
        way = WAYS[i]
        device, inside = neighbour(way)
        source, target = moves[way]
        return pltpu.make_async_remote_copy(
            src_ref=source, dst_ref=target, send_sem=send_sems.at[i], recv_sem=recv_sems.at[i],
            device_id=device, device_id_type=pl.DeviceIdType.MESH), inside

    def start():
        for i in range(len(WAYS)):
            _, inside = neighbour(WAYS[i])

            @pl.when(inside)
            def _(i=i):
                copy(i)[0].start()

    def wait():
        for i in range(len(WAYS)):
            _, behind = neighbour((-WAYS[i][0], -WAYS[i][1]))

            @pl.when(jnp.logical_not(behind))
            def _(i=i):
                target = moves[WAYS[i]][1]
                target[...] = jnp.zeros(target.shape, F32)

        for i in range(len(WAYS)):
            _, inside = neighbour(WAYS[i])
            _, behind = neighbour((-WAYS[i][0], -WAYS[i][1]))

            @pl.when(inside)
            def _(i=i):
                copy(i)[0].wait_send()

            @pl.when(behind)
            def _(i=i):
                copy(i)[0].wait_recv()

    return start, wait


def front_kernel(control_ref, corr_ref, jac_ref,
                 north_ref, south_ref, west_ref, east_ref, g_both, gt_hi, gt_lo,
                 tiles, ends, sides, send_sems, recv_sems, sems):
    rows, cols, _ = control_ref.shape
    loads = [
        pltpu.make_async_copy(control_ref.at[:, pl.ds(0, 8), :], tiles.at[0], sems.at[0]),
        pltpu.make_async_copy(control_ref.at[:, pl.ds(cols - 8, 8), :], tiles.at[1], sems.at[1]),
        pltpu.make_async_copy(control_ref.at[0], ends.at[0], sems.at[2]),
        pltpu.make_async_copy(control_ref.at[rows - 1], ends.at[1], sems.at[3]),
    ]
    for load in loads:
        load.start()
    greet()
    for load in loads:
        load.wait()
    sides[0] = tiles[0, :, 0, :]
    sides[1] = tiles[1, :, 7, :]
    low, high = pl.ds(0, EDGE), pl.ds(rows + EDGE, EDGE)
    first, last = pl.ds(0, EDGE), pl.ds(rows - EDGE, EDGE)
    start_halo, wait_halo = exchange({
        (1, 0): (ends.at[1], north_ref),
        (-1, 0): (ends.at[0], south_ref),
        (0, 1): (sides.at[1], west_ref.at[pl.ds(EDGE, rows), :]),
        (0, -1): (sides.at[0], east_ref.at[pl.ds(EDGE, rows), :]),
        (1, 1): (sides.at[1, last, :], west_ref.at[low, :]),
        (1, -1): (sides.at[0, last, :], east_ref.at[low, :]),
        (-1, 1): (sides.at[1, first, :], west_ref.at[high, :]),
        (-1, -1): (sides.at[0, first, :], east_ref.at[high, :]),
    }, send_sems, recv_sems)
    start_halo()
    for k in range(9):
        g = combined(corr_ref, jac_ref, k)
        hi, lo = split(g)
        g_both[k * 128:(k + 1) * 128, 0:128] = hi
        g_both[k * 128:(k + 1) * 128, 128:256] = lo
        hi, lo = split(g.T)
        for half in range(2):
            gt_hi[half * 128:(half + 1) * 128, k * 128:(k + 1) * 128] = hi
            gt_lo[half * 128:(half + 1) * 128, k * 128:(k + 1) * 128] = lo
    wait_halo()


def back_kernel(out_n, out_s, out_w, out_e, got_n, got_s, got_w, got_e, nw, ne, sw, se, send_sems, recv_sems):
    cols = out_n.shape[0] - 2 * EDGE
    middle, low, high = pl.ds(EDGE, cols), pl.ds(0, EDGE), pl.ds(cols + EDGE, EDGE)
    greet()
    start_edges, wait_edges = exchange({
        (1, 0): (out_s.at[middle, :], got_n),
        (-1, 0): (out_n.at[middle, :], got_s),
        (0, 1): (out_e, got_w),
        (0, -1): (out_w, got_e),
        (1, 1): (out_s.at[high, :], nw),
        (1, -1): (out_s.at[low, :], ne),
        (-1, 1): (out_n.at[high, :], sw),
        (-1, -1): (out_n.at[low, :], se),
    }, send_sems, recv_sems)
    start_edges()
    wait_edges()


def finish_kernel(north_ref, south_ref, west_ref, east_ref, nw_ref, ne_ref, sw_ref, se_ref, grad_in,
                  grad_ref, line_n, line_s, tile_w, tile_e, sems):
    rows, cols, _ = grad_in.shape
    inner = pl.ds(1, rows - 2)
    ends = ((grad_ref.at[0], line_n), (grad_ref.at[rows - 1], line_s),
            (grad_ref.at[inner, pl.ds(0, 8), :], tile_w), (grad_ref.at[inner, pl.ds(cols - 8, 8), :], tile_e))
    loads = [pltpu.make_async_copy(far, near, sems.at[i]) for i, (far, near) in enumerate(ends)]
    for copy in loads:
        copy.start()
    for copy in loads:
        copy.wait()
    line_n[...] += north_ref[...]
    line_s[...] += south_ref[...]
    line_n[0:1, :] += west_ref[0:1, :] + nw_ref[0:1, :]
    line_n[cols - 1:cols, :] += east_ref[0:1, :] + ne_ref[7:8, :]
    line_s[0:1, :] += west_ref[rows - 1:rows, :] + sw_ref[0:1, :]
    line_s[cols - 1:cols, :] += east_ref[rows - 1:rows, :] + se_ref[7:8, :]

    flat_w = tile_w.reshape((rows - 2) * 8, 128)
    flat_e = tile_e.reshape((rows - 2) * 8, 128)
    flat_w[pl.ds(0, rows - 2, stride=8), :] += west_ref[1:rows - 1, :]
    flat_e[pl.ds(7, rows - 2, stride=8), :] += east_ref[1:rows - 1, :]
    stores = [pltpu.make_async_copy(near, far, sems.at[i]) for i, (far, near) in enumerate(ends)]
    for copy in stores:
        copy.start()
    for copy in stores:
        copy.wait()


def body(control, corr_blocks, jacobian, obs_values, obs_count, obs_col, obs_frac, obs_rinv):
    n_devices = lax.axis_size("lat") * lax.axis_size("lon")
    rows, cols, levels = control.shape
    channels = jacobian.shape[1]
    slots = obs_col.shape[1]
    pitch = cols + 2 * EDGE
    vmem = pl.BlockSpec(memory_space=pltpu.VMEM)
    smem = pl.BlockSpec(memory_space=pltpu.SMEM)
    hbm = pl.BlockSpec(memory_space=pl.ANY)

    def to_owners(x):
        blocks = x.reshape(n_devices, CAP, channels)
        return lax.all_to_all(blocks, ("lat", "lon"), split_axis=0, concat_axis=0, tiled=True).reshape(slots, channels)

    observed = to_owners(obs_values)

    def struct(count):
        return jax.ShapeDtypeStruct((count, levels), F32)

    north, south, west, east, g_both, gt_hi, gt_lo = pl.pallas_call(
        front_kernel,
        out_shape=[struct(cols), struct(cols), struct(rows + 2 * EDGE), struct(rows + 2 * EDGE),
                   jax.ShapeDtypeStruct((9 * levels, 2 * channels), BF16),
                   jax.ShapeDtypeStruct((2 * channels, 9 * levels), BF16),
                   jax.ShapeDtypeStruct((2 * channels, 9 * levels), BF16)],
        in_specs=[hbm, vmem, vmem],
        out_specs=[vmem] * 7,
        scratch_shapes=[
            pltpu.VMEM((2, rows, 8, levels), F32),
            pltpu.VMEM((2, cols, levels), F32),
            pltpu.VMEM((2, rows, levels), F32),
            pltpu.SemaphoreType.DMA((8,)),
            pltpu.SemaphoreType.DMA((8,)),
            pltpu.SemaphoreType.DMA((4,)),
        ],
        compiler_params=pltpu.CompilerParams(collective_id=0, has_side_effects=True, vmem_limit_bytes=56 * 2**20),
        name="front",
    )(control, corr_blocks, jacobian)

    chunk_slots = math.gcd(slots, 512)
    limit = pltpu.CompilerParams(vmem_limit_bytes=56 * 2**20)
    weighted, rounded = pl.pallas_call(
        functools.partial(forward_kernel, pitch, chunk_slots),
        out_shape=[jax.ShapeDtypeStruct((slots, channels), F32), jax.ShapeDtypeStruct((slots, channels), BF16)],
        in_specs=[smem, smem] + [vmem] * 8 + [hbm],
        out_specs=[vmem, vmem],
        scratch_shapes=[
            pltpu.VMEM((rows + 2, pitch, levels), F32),
            pltpu.VMEM((ODD * 8, levels), F32),
            pltpu.VMEM((ODD * 8, levels), F32),
            pltpu.VMEM((chunk_slots, levels), F32),
            pltpu.VMEM((chunk_slots, levels), F32),
            pltpu.VMEM((2 * chunk_slots, 9 * levels), BF16),
            pltpu.SemaphoreType.DMA,
        ],
        compiler_params=limit,
        cost_estimate=pl.CostEstimate(flops=2 * slots * 1152 * 512, bytes_accessed=40 * 2**20, transcendentals=0),
        name="forward",
    )(obs_col, obs_count, obs_frac, obs_rinv, observed, g_both, north, south, west, east, control)

    returned = to_owners(rounded)

    gradient, out_n, out_s, out_w, out_e = pl.pallas_call(
        functools.partial(adjoint_kernel, pitch, chunk_slots),
        out_shape=[
            jax.ShapeDtypeStruct(control.shape, F32),
            jax.ShapeDtypeStruct((pitch, levels), F32),
            jax.ShapeDtypeStruct((pitch, levels), F32),
            jax.ShapeDtypeStruct((rows, levels), F32),
            jax.ShapeDtypeStruct((rows, levels), F32),
        ],
        in_specs=[smem] + [vmem] * 4 + [hbm],
        out_specs=[hbm] + [vmem] * 4,
        scratch_shapes=[
            pltpu.VMEM((rows + 2, pitch, levels), F32),
            pltpu.VMEM((ODD * 8, levels), F32),
            pltpu.VMEM((ODD * 8, levels), F32),
            pltpu.VMEM((chunk_slots, levels), F32),
            pltpu.VMEM((chunk_slots, levels), F32),
            pltpu.VMEM((chunk_slots, 9 * levels), F32),
            pltpu.SemaphoreType.DMA,
        ],
        compiler_params=limit,
        cost_estimate=pl.CostEstimate(flops=2 * slots * 1152 * 512, bytes_accessed=60 * 2**20, transcendentals=0),
        name="adjoint",
    )(obs_col, obs_frac, gt_hi, gt_lo, weighted, control)

    got = pl.pallas_call(
        back_kernel,
        out_shape=[struct(cols), struct(cols), struct(rows), struct(rows)] + [struct(EDGE)] * 4,
        in_specs=[vmem] * 4,
        out_specs=[vmem] * 8,
        scratch_shapes=[
            pltpu.SemaphoreType.DMA((8,)),
            pltpu.SemaphoreType.DMA((8,)),
        ],
        compiler_params=pltpu.CompilerParams(collective_id=1, has_side_effects=True),
        name="back",
    )(out_n, out_s, out_w, out_e)
    gradient = pl.pallas_call(
        finish_kernel,
        out_shape=jax.ShapeDtypeStruct(control.shape, F32),
        in_specs=[vmem] * 8 + [hbm],
        out_specs=hbm,
        scratch_shapes=[
            pltpu.VMEM((cols, levels), F32),
            pltpu.VMEM((cols, levels), F32),
            pltpu.VMEM((rows - 2, 8, levels), F32),
            pltpu.VMEM((rows - 2, 8, levels), F32),
            pltpu.SemaphoreType.DMA((4,)),
        ],
        input_output_aliases={8: 0},
        name="finish",
    )(*got, gradient)
    return (gradient, returned)


def solution(mesh):
    in_specs = (
        P("lat", "lon", None),
        P(),
        P(),
        P(("lat", "lon"), None),
        P(("lat", "lon"), None),
        P(("lat", "lon"), None),
        P(("lat", "lon"), None, None),
        P(("lat", "lon"), None),
    )
    out_specs = (P("lat", "lon", None), P(("lat", "lon"), None))
    return jax.shard_map(body, mesh=mesh, in_specs=in_specs, out_specs=out_specs, check_vma=False)
```

```python
import functools
import math
import jax
import jax.numpy as jnp
from jax import lax
from jax.experimental import pallas as pl
from jax.experimental.pallas import tpu as pltpu
from jax.sharding import PartitionSpec as P

CAP = 64
SUB = 128
ODD = 17
CLASH = 1 << 20
EDGE = 8
F32 = jnp.float32
BF16 = jnp.bfloat16
WAYS = ((1, 0), (-1, 0), (0, 1), (0, -1), (1, 1), (1, -1), (-1, 1), (-1, -1))


def split(x):
    hi = x.astype(BF16)
    return hi, (x - hi.astype(F32)).astype(BF16)


def column(row):
    return jnp.broadcast_to(row, (128, SUB)).T


def combined(corr_ref, jac_ref, k):
    return jnp.dot(corr_ref[k], jac_ref[...], precision=lax.Precision.HIGHEST, preferred_element_type=F32)


def entries_of(corner, cols, pitch):
    i, j = corner // cols, corner % cols
    slot = lax.broadcasted_iota(jnp.int32, corner.shape, 1) % 8
    clash = jnp.zeros(corner.shape, jnp.bool_)
    for k in range(1, 8):
        near = (jnp.abs(i - jnp.roll(i, k, axis=1)) < 4) & (jnp.abs(j - jnp.roll(j, k, axis=1)) < 4)
        clash |= near & (slot >= k)
    return i * pitch + j + (EDGE - 1) + jnp.where(clash, CLASH, 0)


def weigh_kernel(count_ref, rinv_ref, observed_ref, evolved_ref, weighted_ref, rounded_ref):
    lane = lax.broadcasted_iota(jnp.int32, (1, SUB), 1)

    def part(m, c):
        at = pl.ds(pl.multiple_of(m * SUB, SUB), SUB)
        live = jnp.zeros((1, SUB), jnp.int32)
        for n in range(SUB // CAP):
            count = count_ref[0, m * (SUB // CAP) + n]
            live += ((lane >= n * CAP) & (lane < n * CAP + count)).astype(jnp.int32)
        rinv = jnp.where(live > 0, rinv_ref[0:1, at], 0.0)
        weighted = column(rinv) * (evolved_ref[at, :] - observed_ref[at, :].astype(F32))
        weighted_ref[at, :] = weighted
        rounded_ref[at, :] = weighted.astype(BF16)
        return c

    lax.fori_loop(0, evolved_ref.shape[0] // SUB, part, 0)


def forward_kernel(pitch, chunk_slots, entry_ref, frac_ref, g_both,
                   north_ref, south_ref, west_ref, east_ref, control_ref, evolved_ref,
                   pad, patches_a, patches_b, f_ref, g_ref, p_both, sem):
    rows, cols, _ = control_ref.shape
    fetch = pltpu.make_async_copy(control_ref, pad.at[pl.ds(1, rows), pl.ds(EDGE, cols), :], sem)
    fetch.start()
    flat = pad.reshape((rows + 2) * pitch, 128)
    pad[0, EDGE:EDGE + cols, :] = north_ref[...]
    pad[rows + 1, EDGE:EDGE + cols, :] = south_ref[...]
    flat[pl.ds(EDGE - 1, rows + 2, stride=pitch), :] = west_ref[EDGE - 1:EDGE + rows + 1, :]
    flat[pl.ds(EDGE + cols, rows + 2, stride=pitch), :] = east_ref[EDGE - 1:EDGE + rows + 1, :]
    fetch.wait()

    def chunk(n, carry):
        first = n * chunk_slots

        for m in range(chunk_slots // SUB):
            at = pl.ds(pl.multiple_of(first + m * SUB, SUB), SUB)
            f_ref[m * SUB:(m + 1) * SUB, :] = column(frac_ref[0, 0:1, at])
            g_ref[m * SUB:(m + 1) * SUB, :] = column(frac_ref[0, 1:2, at])

        def pick(start, patches):
            for v in range(8):
                base = entry_ref[0, first + start + v] & (CLASH - 1)
                for r in range(4):
                    patches[v * ODD + r * 4:v * ODD + r * 4 + 4, :] = flat[pl.ds(base + r * pitch, 4), :]

        def mix(start, patches):
            at = pl.ds(pl.multiple_of(start, 8), 8)
            f, g = f_ref[at, :], g_ref[at, :]
            lines = [[patches[pl.ds(r * 4 + q, 8, stride=ODD), :] for q in range(4)] for r in range(4)]
            mixed = []
            for a in range(3):
                lat = [(1.0 - f) * lines[a][q] + f * lines[a + 1][q] for q in range(4)]
                mixed.extend((1.0 - g) * lat[b] + g * lat[b + 1] for b in range(3))
            return mixed

        def pair(t, c):
            start = t * 16
            upper = mix(start, patches_a)
            pick(start + 8, patches_b)
            lower = mix(start + 8, patches_b)
            pick(jnp.minimum(start + 16, chunk_slots - 8), patches_a)
            hi_at = pl.ds(pl.multiple_of(start, 16), 16)
            lo_at = pl.ds(pl.multiple_of(chunk_slots + start, 16), 16)
            for k in range(9):
                hi, lo = split(jnp.concatenate([upper[k], lower[k]], axis=0))
                p_both[hi_at, k * 128:(k + 1) * 128] = hi
                p_both[lo_at, k * 128:(k + 1) * 128] = lo
            return c

        pick(0, patches_a)
        lax.fori_loop(0, chunk_slots // 16, pair, 0, unroll=2)
        both = jnp.dot(p_both[...], g_both[...], preferred_element_type=F32)
        for m in range(chunk_slots // SUB):
            hi, lo = both[m * SUB:(m + 1) * SUB], both[chunk_slots + m * SUB:chunk_slots + (m + 1) * SUB]
            at = pl.ds(pl.multiple_of(first + m * SUB, SUB), SUB)
            evolved_ref[at, :] = hi[:, 0:128] + (hi[:, 128:256] + lo[:, 0:128] + lo[:, 128:256])
        return carry

    lax.fori_loop(0, entry_ref.shape[1] // chunk_slots, chunk, 0)


def adjoint_kernel(pitch, chunk_slots, entry_ref, frac_ref, gt_hi, gt_lo, weighted_ref, control_ref,
                   grad_ref, north_ref, south_ref, west_ref, east_ref, pad, patches_a, patches_b, f_ref, g_ref, q_ref, sem):
    rows, cols, _ = control_ref.shape
    inner = pad.at[pl.ds(1, rows), pl.ds(EDGE, cols), :]
    fetch = pltpu.make_async_copy(control_ref, inner, sem)
    fetch.start()
    for i in (0, rows + 1):
        pad[i] = jnp.zeros((pitch, 128), F32)

    def clear(i, c):
        pad[pl.ds(i, 1), 0:EDGE, :] = jnp.zeros((1, EDGE, 128), F32)
        pad[pl.ds(i, 1), EDGE + cols:pitch, :] = jnp.zeros((1, pitch - cols - EDGE, 128), F32)
        return c

    lax.fori_loop(1, rows + 1, clear, 0)
    fetch.wait()
    flat = pad.reshape((rows + 2) * pitch, 128)

    def chunk(n, carry):
        first = n * chunk_slots
        w_hi, w_lo = split(weighted_ref[pl.ds(pl.multiple_of(first, chunk_slots), chunk_slots), :])
        w = jnp.concatenate([w_hi, w_lo], axis=1)
        q_ref[...] = (jnp.dot(w, gt_hi[...], preferred_element_type=F32)
                      + jnp.dot(w, gt_lo[...], preferred_element_type=F32))

        for m in range(chunk_slots // SUB):
            at = pl.ds(pl.multiple_of(first + m * SUB, SUB), SUB)
            f_ref[m * SUB:(m + 1) * SUB, :] = column(frac_ref[0, 0:1, at])
            g_ref[m * SUB:(m + 1) * SUB, :] = column(frac_ref[0, 1:2, at])

        def mix(start, patches):
            at = pl.ds(pl.multiple_of(start, 8), 8)
            f, g = f_ref[at, :], g_ref[at, :]
            rest_f, rest_g = 1.0 - f, 1.0 - g
            q = [[q_ref[at, (3 * a + b) * 128:(3 * a + b + 1) * 128] for b in range(3)] for a in range(3)]
            for c in range(4):
                line = []
                for a in range(3):
                    terms = ([rest_g * q[a][c]] if c < 3 else []) + ([g * q[a][c - 1]] if c > 0 else [])
                    line.append(sum(terms[1:], terms[0]))
                for r in range(4):
                    terms = ([rest_f * line[r]] if r < 3 else []) + ([f * line[r - 1]] if r > 0 else [])
                    patches[pl.ds(r * 4 + c, 8, stride=ODD), :] = sum(terms[1:], terms[0])

        def spread(entries, patches, apart):
            def summed(v):
                base = entries[v] & (CLASH - 1)
                return [(pl.ds(base + r * pitch, 4),
                         flat[pl.ds(base + r * pitch, 4), :] + patches[v * ODD + r * 4:v * ODD + r * 4 + 4, :])
                        for r in range(4)]

            for group in ([range(8)] if apart else [[v] for v in range(8)]):
                for where, value in [one for v in group for one in summed(v)]:
                    flat[where, :] = value

        def step(start, patches, later, later_patches):
            entries = [entry_ref[0, first + start + v] for v in range(8)]
            clash = functools.reduce(lambda x, y: x | y, entries) >= CLASH

            @pl.when(jnp.logical_not(clash))
            def _():
                spread(entries, patches, True)
                mix(later, later_patches)

            @pl.when(clash)
            def _():
                spread(entries, patches, False)
                mix(later, later_patches)

        def pair(t, c):
            start = t * 16
            step(start, patches_a, start + 8, patches_b)
            step(start + 8, patches_b, jnp.minimum(start + 16, chunk_slots - 8), patches_a)
            return c

        mix(0, patches_a)
        lax.fori_loop(0, chunk_slots // 16, pair, 0)
        return carry

    lax.fori_loop(0, entry_ref.shape[1] // chunk_slots, chunk, 0)
    send = pltpu.make_async_copy(inner, grad_ref, sem)
    send.start()
    north_ref[...] = pad[0]
    south_ref[...] = pad[rows + 1]
    west_ref[...] = flat[pl.ds(pitch + EDGE - 1, rows, stride=pitch), :]
    east_ref[...] = flat[pl.ds(pitch + EDGE + cols, rows, stride=pitch), :]
    send.wait()


def neighbour(way):
    p = lax.axis_index("lat") + way[0]
    q = lax.axis_index("lon") + way[1]
    inside = (p >= 0) & (p < lax.axis_size("lat")) & (q >= 0) & (q < lax.axis_size("lon"))
    return (p, q), inside


def greet():
    barrier = pltpu.get_barrier_semaphore()
    for way in WAYS:
        device, inside = neighbour(way)

        @pl.when(inside)
        def _(device=device):
            pl.semaphore_signal(barrier, inc=1, device_id=device, device_id_type=pl.DeviceIdType.MESH)

    p, q = lax.axis_index("lat"), lax.axis_index("lon")
    near_lat = jnp.minimum(p + 1, lax.axis_size("lat") - 1) - jnp.maximum(p - 1, 0) + 1
    near_lon = jnp.minimum(q + 1, lax.axis_size("lon") - 1) - jnp.maximum(q - 1, 0) + 1
    pl.semaphore_wait(barrier, near_lat * near_lon - 1)


def exchange(moves, send_sems, recv_sems):
    def copy(i):
        way = WAYS[i]
        device, inside = neighbour(way)
        source, target = moves[way]
        return pltpu.make_async_remote_copy(
            src_ref=source, dst_ref=target, send_sem=send_sems.at[i], recv_sem=recv_sems.at[i],
            device_id=device, device_id_type=pl.DeviceIdType.MESH), inside

    def start():
        for i in range(len(WAYS)):
            _, inside = neighbour(WAYS[i])

            @pl.when(inside)
            def _(i=i):
                copy(i)[0].start()

    def wait():
        for i in range(len(WAYS)):
            _, behind = neighbour((-WAYS[i][0], -WAYS[i][1]))

            @pl.when(jnp.logical_not(behind))
            def _(i=i):
                target = moves[WAYS[i]][1]
                target[...] = jnp.zeros(target.shape, F32)

        for i in range(len(WAYS)):
            _, inside = neighbour(WAYS[i])
            _, behind = neighbour((-WAYS[i][0], -WAYS[i][1]))

            @pl.when(inside)
            def _(i=i):
                copy(i)[0].wait_send()

            @pl.when(behind)
            def _(i=i):
                copy(i)[0].wait_recv()

    return start, wait


def front_kernel(control_ref, corr_ref, jac_ref,
                 north_ref, south_ref, west_ref, east_ref, g_both, gt_hi, gt_lo,
                 tiles, ends, sides, send_sems, recv_sems, sems):
    rows, cols, _ = control_ref.shape
    loads = [
        pltpu.make_async_copy(control_ref.at[:, pl.ds(0, 8), :], tiles.at[0], sems.at[0]),
        pltpu.make_async_copy(control_ref.at[:, pl.ds(cols - 8, 8), :], tiles.at[1], sems.at[1]),
        pltpu.make_async_copy(control_ref.at[0], ends.at[0], sems.at[2]),
        pltpu.make_async_copy(control_ref.at[rows - 1], ends.at[1], sems.at[3]),
    ]
    for load in loads:
        load.start()
    greet()
    for load in loads:
        load.wait()
    sides[0] = tiles[0, :, 0, :]
    sides[1] = tiles[1, :, 7, :]
    low, high = pl.ds(0, EDGE), pl.ds(rows + EDGE, EDGE)
    first, last = pl.ds(0, EDGE), pl.ds(rows - EDGE, EDGE)
    start_halo, wait_halo = exchange({
        (1, 0): (ends.at[1], north_ref),
        (-1, 0): (ends.at[0], south_ref),
        (0, 1): (sides.at[1], west_ref.at[pl.ds(EDGE, rows), :]),
        (0, -1): (sides.at[0], east_ref.at[pl.ds(EDGE, rows), :]),
        (1, 1): (sides.at[1, last, :], west_ref.at[low, :]),
        (1, -1): (sides.at[0, last, :], east_ref.at[low, :]),
        (-1, 1): (sides.at[1, first, :], west_ref.at[high, :]),
        (-1, -1): (sides.at[0, first, :], east_ref.at[high, :]),
    }, send_sems, recv_sems)
    start_halo()
    for k in range(9):
        g = combined(corr_ref, jac_ref, k)
        hi, lo = split(g)
        g_both[k * 128:(k + 1) * 128, 0:128] = hi
        g_both[k * 128:(k + 1) * 128, 128:256] = lo
        hi, lo = split(g.T)
        for half in range(2):
            gt_hi[half * 128:(half + 1) * 128, k * 128:(k + 1) * 128] = hi
            gt_lo[half * 128:(half + 1) * 128, k * 128:(k + 1) * 128] = lo
    wait_halo()


def back_kernel(out_n, out_s, out_w, out_e, got_n, got_s, got_w, got_e, nw, ne, sw, se, send_sems, recv_sems):
    cols = out_n.shape[0] - 2 * EDGE
    middle, low, high = pl.ds(EDGE, cols), pl.ds(0, EDGE), pl.ds(cols + EDGE, EDGE)
    greet()
    start_edges, wait_edges = exchange({
        (1, 0): (out_s.at[middle, :], got_n),
        (-1, 0): (out_n.at[middle, :], got_s),
        (0, 1): (out_e, got_w),
        (0, -1): (out_w, got_e),
        (1, 1): (out_s.at[high, :], nw),
        (1, -1): (out_s.at[low, :], ne),
        (-1, 1): (out_n.at[high, :], sw),
        (-1, -1): (out_n.at[low, :], se),
    }, send_sems, recv_sems)
    start_edges()
    wait_edges()


def finish_kernel(north_ref, south_ref, west_ref, east_ref, nw_ref, ne_ref, sw_ref, se_ref, grad_in,
                  grad_ref, line_n, line_s, tile_w, tile_e, sems):
    rows, cols, _ = grad_in.shape
    inner = pl.ds(1, rows - 2)
    ends = ((grad_ref.at[0], line_n), (grad_ref.at[rows - 1], line_s),
            (grad_ref.at[inner, pl.ds(0, 8), :], tile_w), (grad_ref.at[inner, pl.ds(cols - 8, 8), :], tile_e))
    loads = [pltpu.make_async_copy(far, near, sems.at[i]) for i, (far, near) in enumerate(ends)]
    for copy in loads:
        copy.start()
    for copy in loads:
        copy.wait()
    line_n[...] += north_ref[...]
    line_s[...] += south_ref[...]
    line_n[0:1, :] += west_ref[0:1, :] + nw_ref[0:1, :]
    line_n[cols - 1:cols, :] += east_ref[0:1, :] + ne_ref[7:8, :]
    line_s[0:1, :] += west_ref[rows - 1:rows, :] + sw_ref[0:1, :]
    line_s[cols - 1:cols, :] += east_ref[rows - 1:rows, :] + se_ref[7:8, :]

    flat_w = tile_w.reshape((rows - 2) * 8, 128)
    flat_e = tile_e.reshape((rows - 2) * 8, 128)
    flat_w[pl.ds(0, rows - 2, stride=8), :] += west_ref[1:rows - 1, :]
    flat_e[pl.ds(7, rows - 2, stride=8), :] += east_ref[1:rows - 1, :]
    stores = [pltpu.make_async_copy(near, far, sems.at[i]) for i, (far, near) in enumerate(ends)]
    for copy in stores:
        copy.start()
    for copy in stores:
        copy.wait()


def body(control, corr_blocks, jacobian, obs_values, obs_count, obs_col, obs_frac, obs_rinv):
    n_devices = lax.axis_size("lat") * lax.axis_size("lon")
    rows, cols, levels = control.shape
    channels = jacobian.shape[1]
    slots = obs_col.shape[1]
    pitch = cols + 2 * EDGE
    vmem = pl.BlockSpec(memory_space=pltpu.VMEM)
    smem = pl.BlockSpec(memory_space=pltpu.SMEM)
    hbm = pl.BlockSpec(memory_space=pl.ANY)

    def to_owners(x):
        blocks = x.reshape(n_devices, CAP, channels)
        return lax.all_to_all(blocks, ("lat", "lon"), split_axis=0, concat_axis=0, tiled=True).reshape(slots, channels)

    observed = to_owners(obs_values)

    def struct(count):
        return jax.ShapeDtypeStruct((count, levels), F32)

    north, south, west, east, g_both, gt_hi, gt_lo = pl.pallas_call(
        front_kernel,
        out_shape=[struct(cols), struct(cols), struct(rows + 2 * EDGE), struct(rows + 2 * EDGE),
                   jax.ShapeDtypeStruct((9 * levels, 2 * channels), BF16),
                   jax.ShapeDtypeStruct((2 * channels, 9 * levels), BF16),
                   jax.ShapeDtypeStruct((2 * channels, 9 * levels), BF16)],
        in_specs=[hbm, vmem, vmem],
        out_specs=[vmem] * 7,
        scratch_shapes=[
            pltpu.VMEM((2, rows, 8, levels), F32),
            pltpu.VMEM((2, cols, levels), F32),
            pltpu.VMEM((2, rows, levels), F32),
            pltpu.SemaphoreType.DMA((8,)),
            pltpu.SemaphoreType.DMA((8,)),
            pltpu.SemaphoreType.DMA((4,)),
        ],
        compiler_params=pltpu.CompilerParams(collective_id=0, has_side_effects=True, vmem_limit_bytes=56 * 2**20),
        name="front",
    )(control, corr_blocks, jacobian)

    chunk_slots = math.gcd(slots, 512)
    limit = pltpu.CompilerParams(vmem_limit_bytes=56 * 2**20)
    entries = entries_of(obs_col, cols, pitch)
    evolved = pl.pallas_call(
        functools.partial(forward_kernel, pitch, chunk_slots),
        out_shape=jax.ShapeDtypeStruct((slots, channels), F32),
        in_specs=[smem] + [vmem] * 6 + [hbm],
        out_specs=vmem,
        scratch_shapes=[
            pltpu.VMEM((rows + 2, pitch, levels), F32),
            pltpu.VMEM((ODD * 8, levels), F32),
            pltpu.VMEM((ODD * 8, levels), F32),
            pltpu.VMEM((chunk_slots, levels), F32),
            pltpu.VMEM((chunk_slots, levels), F32),
            pltpu.VMEM((2 * chunk_slots, 9 * levels), BF16),
            pltpu.SemaphoreType.DMA,
        ],
        compiler_params=limit,
        cost_estimate=pl.CostEstimate(flops=2 * slots * 1152 * 512, bytes_accessed=40 * 2**20, transcendentals=0),
        name="forward",
    )(entries, obs_frac, g_both, north, south, west, east, control)

    weighted, rounded = pl.pallas_call(
        weigh_kernel,
        out_shape=[jax.ShapeDtypeStruct((slots, channels), F32), jax.ShapeDtypeStruct((slots, channels), BF16)],
        in_specs=[smem] + [vmem] * 3,
        out_specs=[vmem, vmem],
        compiler_params=limit,
        name="weigh",
    )(obs_count, obs_rinv, observed, evolved)

    returned = to_owners(rounded)

    gradient, out_n, out_s, out_w, out_e = pl.pallas_call(
        functools.partial(adjoint_kernel, pitch, chunk_slots),
        out_shape=[
            jax.ShapeDtypeStruct(control.shape, F32),
            jax.ShapeDtypeStruct((pitch, levels), F32),
            jax.ShapeDtypeStruct((pitch, levels), F32),
            jax.ShapeDtypeStruct((rows, levels), F32),
            jax.ShapeDtypeStruct((rows, levels), F32),
        ],
        in_specs=[smem] + [vmem] * 4 + [hbm],
        out_specs=[hbm] + [vmem] * 4,
        scratch_shapes=[
            pltpu.VMEM((rows + 2, pitch, levels), F32),
            pltpu.VMEM((ODD * 8, levels), F32),
            pltpu.VMEM((ODD * 8, levels), F32),
            pltpu.VMEM((chunk_slots, levels), F32),
            pltpu.VMEM((chunk_slots, levels), F32),
            pltpu.VMEM((chunk_slots, 9 * levels), F32),
            pltpu.SemaphoreType.DMA,
        ],
        compiler_params=limit,
        cost_estimate=pl.CostEstimate(flops=2 * slots * 1152 * 512, bytes_accessed=60 * 2**20, transcendentals=0),
        name="adjoint",
    )(entries, obs_frac, gt_hi, gt_lo, weighted, control)

    got = pl.pallas_call(
        back_kernel,
        out_shape=[struct(cols), struct(cols), struct(rows), struct(rows)] + [struct(EDGE)] * 4,
        in_specs=[vmem] * 4,
        out_specs=[vmem] * 8,
        scratch_shapes=[
            pltpu.SemaphoreType.DMA((8,)),
            pltpu.SemaphoreType.DMA((8,)),
        ],
        compiler_params=pltpu.CompilerParams(collective_id=1, has_side_effects=True),
        name="back",
    )(out_n, out_s, out_w, out_e)
    gradient = pl.pallas_call(
        finish_kernel,
        out_shape=jax.ShapeDtypeStruct(control.shape, F32),
        in_specs=[vmem] * 8 + [hbm],
        out_specs=hbm,
        scratch_shapes=[
            pltpu.VMEM((cols, levels), F32),
            pltpu.VMEM((cols, levels), F32),
            pltpu.VMEM((rows - 2, 8, levels), F32),
            pltpu.VMEM((rows - 2, 8, levels), F32),
            pltpu.SemaphoreType.DMA((4,)),
        ],
        input_output_aliases={8: 0},
        name="finish",
    )(*got, gradient)
    return (gradient, returned)


def solution(mesh):
    in_specs = (
        P("lat", "lon", None),
        P(),
        P(),
        P(("lat", "lon"), None),
        P(("lat", "lon"), None),
        P(("lat", "lon"), None),
        P(("lat", "lon"), None, None),
        P(("lat", "lon"), None),
    )
    out_specs = (P("lat", "lon", None), P(("lat", "lon"), None))
    return jax.shard_map(body, mesh=mesh, in_specs=in_specs, out_specs=out_specs, check_vma=False)
```

```python
import functools
import math
import jax
import jax.numpy as jnp
from jax import lax
from jax.experimental import pallas as pl
from jax.experimental.pallas import tpu as pltpu
from jax.sharding import PartitionSpec as P

CAP = 64
SUB = 128
ODD = 17
EDGE = 8
F32 = jnp.float32
BF16 = jnp.bfloat16
WAYS = ((1, 0), (-1, 0), (0, 1), (0, -1), (1, 1), (1, -1), (-1, 1), (-1, -1))


def split(x):
    hi = x.astype(BF16)
    return hi, (x - hi.astype(F32)).astype(BF16)


def column(row):
    return jnp.broadcast_to(row, (128, SUB)).T


def combined(corr_ref, jac_ref, k):
    return jnp.dot(corr_ref[k], jac_ref[...], precision=lax.Precision.HIGHEST, preferred_element_type=F32)


def place(corner, cols, pitch):
    if cols & (cols - 1) == 0:
        line = lax.shift_right_logical(corner, cols.bit_length() - 1)
    else:
        line = lax.div(corner, cols)
    return corner + line * (pitch - cols) + (EDGE - 1)


def forward_kernel(pitch, chunk_slots, col_ref, frac_ref, g_both,
                   north_ref, south_ref, west_ref, east_ref, control_ref, evolved_ref,
                   pad, patches_a, patches_b, f_ref, g_ref, p_both, sem):
    rows, cols, _ = control_ref.shape
    fetch = pltpu.make_async_copy(control_ref, pad.at[pl.ds(1, rows), pl.ds(EDGE, cols), :], sem)
    fetch.start()
    flat = pad.reshape((rows + 2) * pitch, 128)
    pad[0, EDGE:EDGE + cols, :] = north_ref[...]
    pad[rows + 1, EDGE:EDGE + cols, :] = south_ref[...]
    flat[pl.ds(EDGE - 1, rows + 2, stride=pitch), :] = west_ref[EDGE - 1:EDGE + rows + 1, :]
    flat[pl.ds(EDGE + cols, rows + 2, stride=pitch), :] = east_ref[EDGE - 1:EDGE + rows + 1, :]
    fetch.wait()

    def chunk(n, carry):
        first = n * chunk_slots

        for m in range(chunk_slots // SUB):
            at = pl.ds(pl.multiple_of(first + m * SUB, SUB), SUB)
            f_ref[m * SUB:(m + 1) * SUB, :] = column(frac_ref[0, 0:1, at])
            g_ref[m * SUB:(m + 1) * SUB, :] = column(frac_ref[0, 1:2, at])

        def pick(start, patches):
            for v in range(8):
                base = place(col_ref[0, first + start + v], cols, pitch)
                for r in range(4):
                    patches[v * ODD + r * 4:v * ODD + r * 4 + 4, :] = flat[pl.ds(base + r * pitch, 4), :]

        def mix(start, patches):
            at = pl.ds(pl.multiple_of(start, 8), 8)
            f, g = f_ref[at, :], g_ref[at, :]
            lines = [[patches[pl.ds(r * 4 + q, 8, stride=ODD), :] for q in range(4)] for r in range(4)]
            mixed = []
            for a in range(3):
                lat = [(1.0 - f) * lines[a][q] + f * lines[a + 1][q] for q in range(4)]
                mixed.extend((1.0 - g) * lat[b] + g * lat[b + 1] for b in range(3))
            return mixed

        def pair(t, c):
            start = t * 16
            upper = mix(start, patches_a)
            pick(start + 8, patches_b)
            lower = mix(start + 8, patches_b)
            pick(jnp.minimum(start + 16, chunk_slots - 8), patches_a)
            hi_at = pl.ds(pl.multiple_of(start, 16), 16)
            lo_at = pl.ds(pl.multiple_of(chunk_slots + start, 16), 16)
            for k in range(9):
                hi, lo = split(jnp.concatenate([upper[k], lower[k]], axis=0))
                p_both[hi_at, k * 128:(k + 1) * 128] = hi
                p_both[lo_at, k * 128:(k + 1) * 128] = lo
            return c

        pick(0, patches_a)
        lax.fori_loop(0, chunk_slots // 16, pair, 0, unroll=2)
        both = jnp.dot(p_both[...], g_both[...], preferred_element_type=F32)
        for m in range(chunk_slots // SUB):
            hi, lo = both[m * SUB:(m + 1) * SUB], both[chunk_slots + m * SUB:chunk_slots + (m + 1) * SUB]
            at = pl.ds(pl.multiple_of(first + m * SUB, SUB), SUB)
            evolved_ref[at, :] = hi[:, 0:128] + (hi[:, 128:256] + lo[:, 0:128] + lo[:, 128:256])
        return carry

    lax.fori_loop(0, col_ref.shape[1] // chunk_slots, chunk, 0)


def adjoint_kernel(pitch, chunk_slots, col_ref, frac_ref, gt_hi, gt_lo, weighted_ref, control_ref,
                   grad_ref, north_ref, south_ref, west_ref, east_ref, pad, patches_a, patches_b, f_ref, g_ref, q_ref, sem):
    rows, cols, _ = control_ref.shape
    inner = pad.at[pl.ds(1, rows), pl.ds(EDGE, cols), :]
    fetch = pltpu.make_async_copy(control_ref, inner, sem)
    fetch.start()
    for i in (0, rows + 1):
        pad[i] = jnp.zeros((pitch, 128), F32)

    def clear(i, c):
        pad[pl.ds(i, 1), 0:EDGE, :] = jnp.zeros((1, EDGE, 128), F32)
        pad[pl.ds(i, 1), EDGE + cols:pitch, :] = jnp.zeros((1, pitch - cols - EDGE, 128), F32)
        return c

    lax.fori_loop(1, rows + 1, clear, 0)
    flat = pad.reshape((rows + 2) * pitch, 128)

    def chunk(n, carry):
        first = n * chunk_slots
        w_hi, w_lo = split(weighted_ref[pl.ds(pl.multiple_of(first, chunk_slots), chunk_slots), :])
        w = jnp.concatenate([w_hi, w_lo], axis=1)
        q_ref[...] = (jnp.dot(w, gt_hi[...], preferred_element_type=F32)
                      + jnp.dot(w, gt_lo[...], preferred_element_type=F32))

        for m in range(chunk_slots // SUB):
            at = pl.ds(pl.multiple_of(first + m * SUB, SUB), SUB)
            f_ref[m * SUB:(m + 1) * SUB, :] = column(frac_ref[0, 0:1, at])
            g_ref[m * SUB:(m + 1) * SUB, :] = column(frac_ref[0, 1:2, at])

        def mix(start, patches):
            at = pl.ds(pl.multiple_of(start, 8), 8)
            f, g = f_ref[at, :], g_ref[at, :]
            rest_f, rest_g = 1.0 - f, 1.0 - g
            q = [[q_ref[at, (3 * a + b) * 128:(3 * a + b + 1) * 128] for b in range(3)] for a in range(3)]
            for c in range(4):
                line = []
                for a in range(3):
                    terms = ([rest_g * q[a][c]] if c < 3 else []) + ([g * q[a][c - 1]] if c > 0 else [])
                    line.append(sum(terms[1:], terms[0]))
                for r in range(4):
                    terms = ([rest_f * line[r]] if r < 3 else []) + ([f * line[r - 1]] if r > 0 else [])
                    patches[pl.ds(r * 4 + c, 8, stride=ODD), :] = sum(terms[1:], terms[0])

        def spread(start, patches):
            for v in range(8):
                base = place(col_ref[0, first + start + v], cols, pitch)
                lines = [flat[pl.ds(base + r * pitch, 4), :] + patches[v * ODD + r * 4:v * ODD + r * 4 + 4, :]
                         for r in range(4)]
                for r in range(4):
                    flat[pl.ds(base + r * pitch, 4), :] = lines[r]

        def pair(t, c):
            start = t * 16
            mix(start + 8, patches_b)
            spread(start, patches_a)
            mix(jnp.minimum(start + 16, chunk_slots - 8), patches_a)
            spread(start + 8, patches_b)
            return c

        mix(0, patches_a)

        @pl.when(n == 0)
        def _():
            fetch.wait()

        lax.fori_loop(0, chunk_slots // 16, pair, 0, unroll=2)
        return carry

    lax.fori_loop(0, col_ref.shape[1] // chunk_slots, chunk, 0)
    send = pltpu.make_async_copy(inner, grad_ref, sem)
    send.start()
    north_ref[...] = pad[0]
    south_ref[...] = pad[rows + 1]
    west_ref[...] = flat[pl.ds(pitch + EDGE - 1, rows, stride=pitch), :]
    east_ref[...] = flat[pl.ds(pitch + EDGE + cols, rows, stride=pitch), :]
    send.wait()


def neighbour(way):
    p = lax.axis_index("lat") + way[0]
    q = lax.axis_index("lon") + way[1]
    inside = (p >= 0) & (p < lax.axis_size("lat")) & (q >= 0) & (q < lax.axis_size("lon"))
    return (p, q), inside


def greet():
    barrier = pltpu.get_barrier_semaphore()
    for way in WAYS:
        device, inside = neighbour(way)

        @pl.when(inside)
        def _(device=device):
            pl.semaphore_signal(barrier, inc=1, device_id=device, device_id_type=pl.DeviceIdType.MESH)

    p, q = lax.axis_index("lat"), lax.axis_index("lon")
    near_lat = jnp.minimum(p + 1, lax.axis_size("lat") - 1) - jnp.maximum(p - 1, 0) + 1
    near_lon = jnp.minimum(q + 1, lax.axis_size("lon") - 1) - jnp.maximum(q - 1, 0) + 1
    pl.semaphore_wait(barrier, near_lat * near_lon - 1)


def exchange(moves, send_sems, recv_sems):
    def copy(i):
        way = WAYS[i]
        device, inside = neighbour(way)
        source, target = moves[way]
        return pltpu.make_async_remote_copy(
            src_ref=source, dst_ref=target, send_sem=send_sems.at[i], recv_sem=recv_sems.at[i],
            device_id=device, device_id_type=pl.DeviceIdType.MESH), inside

    def start():
        for i in range(len(WAYS)):
            _, inside = neighbour(WAYS[i])

            @pl.when(inside)
            def _(i=i):
                copy(i)[0].start()

    def wait():
        for i in range(len(WAYS)):
            _, behind = neighbour((-WAYS[i][0], -WAYS[i][1]))

            @pl.when(jnp.logical_not(behind))
            def _(i=i):
                target = moves[WAYS[i]][1]
                target[...] = jnp.zeros(target.shape, F32)

        for i in range(len(WAYS)):
            _, inside = neighbour(WAYS[i])
            _, behind = neighbour((-WAYS[i][0], -WAYS[i][1]))

            @pl.when(inside)
            def _(i=i):
                copy(i)[0].wait_send()

            @pl.when(behind)
            def _(i=i):
                copy(i)[0].wait_recv()

    return start, wait


def front_kernel(control_ref, corr_ref, jac_ref,
                 north_ref, south_ref, west_ref, east_ref, g_both, gt_hi, gt_lo,
                 tiles, ends, sides, send_sems, recv_sems, sems):
    rows, cols, _ = control_ref.shape
    loads = [
        pltpu.make_async_copy(control_ref.at[:, pl.ds(0, 8), :], tiles.at[0], sems.at[0]),
        pltpu.make_async_copy(control_ref.at[:, pl.ds(cols - 8, 8), :], tiles.at[1], sems.at[1]),
        pltpu.make_async_copy(control_ref.at[0], ends.at[0], sems.at[2]),
        pltpu.make_async_copy(control_ref.at[rows - 1], ends.at[1], sems.at[3]),
    ]
    for load in loads:
        load.start()
    greet()
    for load in loads:
        load.wait()
    sides[0] = tiles[0, :, 0, :]
    sides[1] = tiles[1, :, 7, :]
    low, high = pl.ds(0, EDGE), pl.ds(rows + EDGE, EDGE)
    first, last = pl.ds(0, EDGE), pl.ds(rows - EDGE, EDGE)
    start_halo, wait_halo = exchange({
        (1, 0): (ends.at[1], north_ref),
        (-1, 0): (ends.at[0], south_ref),
        (0, 1): (sides.at[1], west_ref.at[pl.ds(EDGE, rows), :]),
        (0, -1): (sides.at[0], east_ref.at[pl.ds(EDGE, rows), :]),
        (1, 1): (sides.at[1, last, :], west_ref.at[low, :]),
        (1, -1): (sides.at[0, last, :], east_ref.at[low, :]),
        (-1, 1): (sides.at[1, first, :], west_ref.at[high, :]),
        (-1, -1): (sides.at[0, first, :], east_ref.at[high, :]),
    }, send_sems, recv_sems)
    start_halo()
    for k in range(9):
        g = combined(corr_ref, jac_ref, k)
        hi, lo = split(g)
        g_both[k * 128:(k + 1) * 128, 0:128] = hi
        g_both[k * 128:(k + 1) * 128, 128:256] = lo
        hi, lo = split(g.T)
        for half in range(2):
            gt_hi[half * 128:(half + 1) * 128, k * 128:(k + 1) * 128] = hi
            gt_lo[half * 128:(half + 1) * 128, k * 128:(k + 1) * 128] = lo
    wait_halo()


def back_kernel(out_n, out_s, out_w, out_e, got_n, got_s, got_w, got_e, nw, ne, sw, se, send_sems, recv_sems):
    cols = out_n.shape[0] - 2 * EDGE
    middle, low, high = pl.ds(EDGE, cols), pl.ds(0, EDGE), pl.ds(cols + EDGE, EDGE)
    greet()
    start_edges, wait_edges = exchange({
        (1, 0): (out_s.at[middle, :], got_n),
        (-1, 0): (out_n.at[middle, :], got_s),
        (0, 1): (out_e, got_w),
        (0, -1): (out_w, got_e),
        (1, 1): (out_s.at[high, :], nw),
        (1, -1): (out_s.at[low, :], ne),
        (-1, 1): (out_n.at[high, :], sw),
        (-1, -1): (out_n.at[low, :], se),
    }, send_sems, recv_sems)
    start_edges()
    wait_edges()


def finish_kernel(north_ref, south_ref, west_ref, east_ref, nw_ref, ne_ref, sw_ref, se_ref, grad_in,
                  grad_ref, line_n, line_s, tile_w, tile_e, sems):
    rows, cols, _ = grad_in.shape
    inner = pl.ds(1, rows - 2)
    ends = ((grad_ref.at[0], line_n), (grad_ref.at[rows - 1], line_s),
            (grad_ref.at[inner, pl.ds(0, 8), :], tile_w), (grad_ref.at[inner, pl.ds(cols - 8, 8), :], tile_e))
    loads = [pltpu.make_async_copy(far, near, sems.at[i]) for i, (far, near) in enumerate(ends)]
    for copy in loads:
        copy.start()
    for copy in loads:
        copy.wait()
    line_n[...] += north_ref[...]
    line_s[...] += south_ref[...]
    line_n[0:1, :] += west_ref[0:1, :] + nw_ref[0:1, :]
    line_n[cols - 1:cols, :] += east_ref[0:1, :] + ne_ref[7:8, :]
    line_s[0:1, :] += west_ref[rows - 1:rows, :] + sw_ref[0:1, :]
    line_s[cols - 1:cols, :] += east_ref[rows - 1:rows, :] + se_ref[7:8, :]

    flat_w = tile_w.reshape((rows - 2) * 8, 128)
    flat_e = tile_e.reshape((rows - 2) * 8, 128)
    flat_w[pl.ds(0, rows - 2, stride=8), :] += west_ref[1:rows - 1, :]
    flat_e[pl.ds(7, rows - 2, stride=8), :] += east_ref[1:rows - 1, :]
    stores = [pltpu.make_async_copy(near, far, sems.at[i]) for i, (far, near) in enumerate(ends)]
    for copy in stores:
        copy.start()
    for copy in stores:
        copy.wait()


def body(control, corr_blocks, jacobian, obs_values, obs_count, obs_col, obs_frac, obs_rinv):
    n_devices = lax.axis_size("lat") * lax.axis_size("lon")
    rows, cols, levels = control.shape
    channels = jacobian.shape[1]
    slots = obs_col.shape[1]
    pitch = cols + 2 * EDGE
    vmem = pl.BlockSpec(memory_space=pltpu.VMEM)
    smem = pl.BlockSpec(memory_space=pltpu.SMEM)
    hbm = pl.BlockSpec(memory_space=pl.ANY)

    def to_owners(x):
        blocks = x.reshape(n_devices, CAP, channels)
        return lax.all_to_all(blocks, ("lat", "lon"), split_axis=0, concat_axis=0, tiled=True).reshape(slots, channels)

    observed = to_owners(obs_values)

    def struct(count):
        return jax.ShapeDtypeStruct((count, levels), F32)

    north, south, west, east, g_both, gt_hi, gt_lo = pl.pallas_call(
        front_kernel,
        out_shape=[struct(cols), struct(cols), struct(rows + 2 * EDGE), struct(rows + 2 * EDGE),
                   jax.ShapeDtypeStruct((9 * levels, 2 * channels), BF16),
                   jax.ShapeDtypeStruct((2 * channels, 9 * levels), BF16),
                   jax.ShapeDtypeStruct((2 * channels, 9 * levels), BF16)],
        in_specs=[hbm, vmem, vmem],
        out_specs=[vmem] * 7,
        scratch_shapes=[
            pltpu.VMEM((2, rows, 8, levels), F32),
            pltpu.VMEM((2, cols, levels), F32),
            pltpu.VMEM((2, rows, levels), F32),
            pltpu.SemaphoreType.DMA((8,)),
            pltpu.SemaphoreType.DMA((8,)),
            pltpu.SemaphoreType.DMA((4,)),
        ],
        compiler_params=pltpu.CompilerParams(collective_id=0, has_side_effects=True, vmem_limit_bytes=56 * 2**20),
        name="front",
    )(control, corr_blocks, jacobian)

    chunk_slots = math.gcd(slots, 512)
    limit = pltpu.CompilerParams(vmem_limit_bytes=56 * 2**20)
    evolved = pl.pallas_call(
        functools.partial(forward_kernel, pitch, chunk_slots),
        out_shape=jax.ShapeDtypeStruct((slots, channels), F32),
        in_specs=[smem] + [vmem] * 6 + [hbm],
        out_specs=vmem,
        scratch_shapes=[
            pltpu.VMEM((rows + 2, pitch, levels), F32),
            pltpu.VMEM((ODD * 8, levels), F32),
            pltpu.VMEM((ODD * 8, levels), F32),
            pltpu.VMEM((chunk_slots, levels), F32),
            pltpu.VMEM((chunk_slots, levels), F32),
            pltpu.VMEM((2 * chunk_slots, 9 * levels), BF16),
            pltpu.SemaphoreType.DMA,
        ],
        compiler_params=limit,
        cost_estimate=pl.CostEstimate(flops=2 * slots * 1152 * 512, bytes_accessed=40 * 2**20, transcendentals=0),
        name="forward",
    )(obs_col, obs_frac, g_both, north, south, west, east, control)

    live = (jnp.arange(CAP, dtype=jnp.int32)[None, :] < obs_count[0][:, None]).reshape(slots, 1)
    departure = evolved - observed.astype(F32)
    weighted = jnp.where(live, obs_rinv[0][:, None] * departure, jnp.zeros_like(departure))
    rounded = weighted.astype(BF16)

    returned = to_owners(rounded)

    gradient, out_n, out_s, out_w, out_e = pl.pallas_call(
        functools.partial(adjoint_kernel, pitch, chunk_slots),
        out_shape=[
            jax.ShapeDtypeStruct(control.shape, F32),
            jax.ShapeDtypeStruct((pitch, levels), F32),
            jax.ShapeDtypeStruct((pitch, levels), F32),
            jax.ShapeDtypeStruct((rows, levels), F32),
            jax.ShapeDtypeStruct((rows, levels), F32),
        ],
        in_specs=[smem] + [vmem] * 4 + [hbm],
        out_specs=[hbm] + [vmem] * 4,
        scratch_shapes=[
            pltpu.VMEM((rows + 2, pitch, levels), F32),
            pltpu.VMEM((ODD * 8, levels), F32),
            pltpu.VMEM((ODD * 8, levels), F32),
            pltpu.VMEM((chunk_slots, levels), F32),
            pltpu.VMEM((chunk_slots, levels), F32),
            pltpu.VMEM((chunk_slots, 9 * levels), F32),
            pltpu.SemaphoreType.DMA,
        ],
        compiler_params=limit,
        cost_estimate=pl.CostEstimate(flops=2 * slots * 1152 * 512, bytes_accessed=60 * 2**20, transcendentals=0),
        name="adjoint",
    )(obs_col, obs_frac, gt_hi, gt_lo, weighted, control)

    got = pl.pallas_call(
        back_kernel,
        out_shape=[struct(cols), struct(cols), struct(rows), struct(rows)] + [struct(EDGE)] * 4,
        in_specs=[vmem] * 4,
        out_specs=[vmem] * 8,
        scratch_shapes=[
            pltpu.SemaphoreType.DMA((8,)),
            pltpu.SemaphoreType.DMA((8,)),
        ],
        compiler_params=pltpu.CompilerParams(collective_id=1, has_side_effects=True),
        name="back",
    )(out_n, out_s, out_w, out_e)
    gradient = pl.pallas_call(
        finish_kernel,
        out_shape=jax.ShapeDtypeStruct(control.shape, F32),
        in_specs=[vmem] * 8 + [hbm],
        out_specs=hbm,
        scratch_shapes=[
            pltpu.VMEM((cols, levels), F32),
            pltpu.VMEM((cols, levels), F32),
            pltpu.VMEM((rows - 2, 8, levels), F32),
            pltpu.VMEM((rows - 2, 8, levels), F32),
            pltpu.SemaphoreType.DMA((4,)),
        ],
        input_output_aliases={8: 0},
        name="finish",
    )(*got, gradient)
    return (gradient, returned)


def solution(mesh):
    in_specs = (
        P("lat", "lon", None),
        P(),
        P(),
        P(("lat", "lon"), None),
        P(("lat", "lon"), None),
        P(("lat", "lon"), None),
        P(("lat", "lon"), None, None),
        P(("lat", "lon"), None),
    )
    out_specs = (P("lat", "lon", None), P(("lat", "lon"), None))
    return jax.shard_map(body, mesh=mesh, in_specs=in_specs, out_specs=out_specs, check_vma=False)
```

```python
import functools
import math
import jax
import jax.numpy as jnp
from jax import lax
from jax.experimental import pallas as pl
from jax.experimental.pallas import tpu as pltpu
from jax.sharding import PartitionSpec as P

CAP = 64
SUB = 128
ODD = 17
EDGE = 8
F32 = jnp.float32
BF16 = jnp.bfloat16
WAYS = ((1, 0), (-1, 0), (0, 1), (0, -1), (1, 1), (1, -1), (-1, 1), (-1, -1))


def split(x):
    hi = x.astype(BF16)
    return hi, (x - hi.astype(F32)).astype(BF16)


def column(row):
    return jnp.broadcast_to(row, (128, SUB)).T


def combined(corr_ref, jac_ref, k):
    return jnp.dot(corr_ref[k], jac_ref[...], precision=lax.Precision.HIGHEST, preferred_element_type=F32)


def place(corner, cols, pitch):
    if cols & (cols - 1) == 0:
        line = lax.shift_right_logical(corner, cols.bit_length() - 1)
    else:
        line = lax.div(corner, cols)
    return corner + line * (pitch - cols) + (EDGE - 1)


def forward_kernel(pitch, chunk_slots, col_ref, count_ref, frac_ref, rinv_ref, observed_ref, g_both,
                   north_ref, south_ref, west_ref, east_ref, control_ref, weighted_ref, rounded_ref,
                   pad, patches_a, patches_b, f_ref, g_ref, p_both, sem):
    rows, cols, _ = control_ref.shape
    fetch = pltpu.make_async_copy(control_ref, pad.at[pl.ds(1, rows), pl.ds(EDGE, cols), :], sem)
    fetch.start()
    flat = pad.reshape((rows + 2) * pitch, 128)
    pad[0, EDGE:EDGE + cols, :] = north_ref[...]
    pad[rows + 1, EDGE:EDGE + cols, :] = south_ref[...]
    flat[pl.ds(EDGE - 1, rows + 2, stride=pitch), :] = west_ref[EDGE - 1:EDGE + rows + 1, :]
    flat[pl.ds(EDGE + cols, rows + 2, stride=pitch), :] = east_ref[EDGE - 1:EDGE + rows + 1, :]
    fetch.wait()

    def chunk(n, carry):
        first = n * chunk_slots

        for m in range(chunk_slots // SUB):
            at = pl.ds(pl.multiple_of(first + m * SUB, SUB), SUB)
            f_ref[m * SUB:(m + 1) * SUB, :] = column(frac_ref[0, 0:1, at])
            g_ref[m * SUB:(m + 1) * SUB, :] = column(frac_ref[0, 1:2, at])

        def pick(start, patches):
            for v in range(8):
                base = place(col_ref[0, first + start + v], cols, pitch)
                for r in range(4):
                    patches[v * ODD + r * 4:v * ODD + r * 4 + 4, :] = flat[pl.ds(base + r * pitch, 4), :]

        def mix(start, patches):
            at = pl.ds(pl.multiple_of(start, 8), 8)
            f, g = f_ref[at, :], g_ref[at, :]
            lines = [[patches[pl.ds(r * 4 + q, 8, stride=ODD), :] for q in range(4)] for r in range(4)]
            mixed = []
            for a in range(3):
                lat = [(1.0 - f) * lines[a][q] + f * lines[a + 1][q] for q in range(4)]
                mixed.extend((1.0 - g) * lat[b] + g * lat[b + 1] for b in range(3))
            return mixed

        def pair(t, c):
            start = t * 16
            upper = mix(start, patches_a)
            pick(start + 8, patches_b)
            lower = mix(start + 8, patches_b)
            pick(jnp.minimum(start + 16, chunk_slots - 8), patches_a)
            hi_at = pl.ds(pl.multiple_of(start, 16), 16)
            lo_at = pl.ds(pl.multiple_of(chunk_slots + start, 16), 16)
            for k in range(9):
                hi, lo = split(jnp.concatenate([upper[k], lower[k]], axis=0))
                p_both[hi_at, k * 128:(k + 1) * 128] = hi
                p_both[lo_at, k * 128:(k + 1) * 128] = lo
            return c

        pick(0, patches_a)
        lax.fori_loop(0, chunk_slots // 16, pair, 0, unroll=2)
        both = jnp.dot(p_both[...], g_both[...], preferred_element_type=F32)
        for m in range(chunk_slots // SUB):
            hi, lo = both[m * SUB:(m + 1) * SUB], both[chunk_slots + m * SUB:chunk_slots + (m + 1) * SUB]
            evolved = hi[:, 0:128] + (hi[:, 128:256] + lo[:, 0:128] + lo[:, 128:256])
            start = pl.multiple_of(first + m * SUB, SUB)
            at = pl.ds(start, SUB)
            lane = lax.broadcasted_iota(jnp.int32, (1, SUB), 1)
            live = jnp.zeros((1, SUB), jnp.int32)
            for part in range(SUB // CAP):
                count = count_ref[0, n * (chunk_slots // CAP) + m * (SUB // CAP) + part]
                live += ((lane >= part * CAP) & (lane < part * CAP + count)).astype(jnp.int32)
            rinv = jnp.where(live > 0, rinv_ref[0:1, at], 0.0)
            weighted = column(rinv) * (evolved - observed_ref[at, :].astype(F32))
            weighted_ref[at, :] = weighted
            rounded_ref[at, :] = weighted.astype(BF16)
        return carry

    lax.fori_loop(0, col_ref.shape[1] // chunk_slots, chunk, 0)


def adjoint_kernel(pitch, chunk_slots, col_ref, frac_ref, gt_hi, gt_lo, weighted_ref, control_ref,
                   grad_ref, north_ref, south_ref, west_ref, east_ref, pad, patches_a, patches_b, f_ref, g_ref, q_ref, sem):
    rows, cols, _ = control_ref.shape
    inner = pad.at[pl.ds(1, rows), pl.ds(EDGE, cols), :]
    fetch = pltpu.make_async_copy(control_ref, inner, sem)
    fetch.start()
    for i in (0, rows + 1):
        pad[i] = jnp.zeros((pitch, 128), F32)

    def clear(i, c):
        pad[pl.ds(i, 1), 0:EDGE, :] = jnp.zeros((1, EDGE, 128), F32)
        pad[pl.ds(i, 1), EDGE + cols:pitch, :] = jnp.zeros((1, pitch - cols - EDGE, 128), F32)
        return c

    lax.fori_loop(1, rows + 1, clear, 0)
    flat = pad.reshape((rows + 2) * pitch, 128)

    def chunk(n, carry):
        first = n * chunk_slots
        w_hi, w_lo = split(weighted_ref[pl.ds(pl.multiple_of(first, chunk_slots), chunk_slots), :])
        w = jnp.concatenate([w_hi, w_lo], axis=1)
        q_ref[...] = (jnp.dot(w, gt_hi[...], preferred_element_type=F32)
                      + jnp.dot(w, gt_lo[...], preferred_element_type=F32))

        for m in range(chunk_slots // SUB):
            at = pl.ds(pl.multiple_of(first + m * SUB, SUB), SUB)
            f_ref[m * SUB:(m + 1) * SUB, :] = column(frac_ref[0, 0:1, at])
            g_ref[m * SUB:(m + 1) * SUB, :] = column(frac_ref[0, 1:2, at])

        def mix(start, patches):
            at = pl.ds(pl.multiple_of(start, 8), 8)
            f, g = f_ref[at, :], g_ref[at, :]
            rest_f, rest_g = 1.0 - f, 1.0 - g
            q = [[q_ref[at, (3 * a + b) * 128:(3 * a + b + 1) * 128] for b in range(3)] for a in range(3)]
            for c in range(4):
                line = []
                for a in range(3):
                    terms = ([rest_g * q[a][c]] if c < 3 else []) + ([g * q[a][c - 1]] if c > 0 else [])
                    line.append(sum(terms[1:], terms[0]))
                for r in range(4):
                    terms = ([rest_f * line[r]] if r < 3 else []) + ([f * line[r - 1]] if r > 0 else [])
                    patches[pl.ds(r * 4 + c, 8, stride=ODD), :] = sum(terms[1:], terms[0])

        def spread(start, patches):
            for v in range(8):
                base = place(col_ref[0, first + start + v], cols, pitch)
                lines = [flat[pl.ds(base + r * pitch, 4), :] + patches[v * ODD + r * 4:v * ODD + r * 4 + 4, :]
                         for r in range(4)]
                for r in range(4):
                    flat[pl.ds(base + r * pitch, 4), :] = lines[r]

        def pair(t, c):
            start = t * 16
            mix(start + 8, patches_b)
            spread(start, patches_a)
            mix(jnp.minimum(start + 16, chunk_slots - 8), patches_a)
            spread(start + 8, patches_b)
            return c

        mix(0, patches_a)

        @pl.when(n == 0)
        def _():
            fetch.wait()

        lax.fori_loop(0, chunk_slots // 16, pair, 0, unroll=2)
        return carry

    lax.fori_loop(0, col_ref.shape[1] // chunk_slots, chunk, 0)
    send = pltpu.make_async_copy(inner, grad_ref, sem)
    send.start()
    north_ref[...] = pad[0]
    south_ref[...] = pad[rows + 1]
    west_ref[...] = flat[pl.ds(pitch + EDGE - 1, rows, stride=pitch), :]
    east_ref[...] = flat[pl.ds(pitch + EDGE + cols, rows, stride=pitch), :]
    send.wait()


def neighbour(way):
    p = lax.axis_index("lat") + way[0]
    q = lax.axis_index("lon") + way[1]
    inside = (p >= 0) & (p < lax.axis_size("lat")) & (q >= 0) & (q < lax.axis_size("lon"))
    return (p, q), inside


def greet():
    barrier = pltpu.get_barrier_semaphore()
    for way in WAYS:
        device, inside = neighbour(way)

        @pl.when(inside)
        def _(device=device):
            pl.semaphore_signal(barrier, inc=1, device_id=device, device_id_type=pl.DeviceIdType.MESH)

    p, q = lax.axis_index("lat"), lax.axis_index("lon")
    near_lat = jnp.minimum(p + 1, lax.axis_size("lat") - 1) - jnp.maximum(p - 1, 0) + 1
    near_lon = jnp.minimum(q + 1, lax.axis_size("lon") - 1) - jnp.maximum(q - 1, 0) + 1
    pl.semaphore_wait(barrier, near_lat * near_lon - 1)


def exchange(moves, send_sems, recv_sems):
    def copy(i):
        way = WAYS[i]
        device, inside = neighbour(way)
        source, target = moves[way]
        return pltpu.make_async_remote_copy(
            src_ref=source, dst_ref=target, send_sem=send_sems.at[i], recv_sem=recv_sems.at[i],
            device_id=device, device_id_type=pl.DeviceIdType.MESH), inside

    def start():
        for i in range(len(WAYS)):
            _, inside = neighbour(WAYS[i])

            @pl.when(inside)
            def _(i=i):
                copy(i)[0].start()

    def wait():
        for i in range(len(WAYS)):
            _, behind = neighbour((-WAYS[i][0], -WAYS[i][1]))

            @pl.when(jnp.logical_not(behind))
            def _(i=i):
                target = moves[WAYS[i]][1]
                target[...] = jnp.zeros(target.shape, F32)

        for i in range(len(WAYS)):
            _, inside = neighbour(WAYS[i])
            _, behind = neighbour((-WAYS[i][0], -WAYS[i][1]))

            @pl.when(inside)
            def _(i=i):
                copy(i)[0].wait_send()

            @pl.when(behind)
            def _(i=i):
                copy(i)[0].wait_recv()

    return start, wait


def front_kernel(control_ref, corr_ref, jac_ref,
                 north_ref, south_ref, west_ref, east_ref, g_both, gt_hi, gt_lo,
                 tiles, ends, sides, send_sems, recv_sems, sems):
    rows, cols, _ = control_ref.shape
    loads = [
        pltpu.make_async_copy(control_ref.at[:, pl.ds(0, 8), :], tiles.at[0], sems.at[0]),
        pltpu.make_async_copy(control_ref.at[:, pl.ds(cols - 8, 8), :], tiles.at[1], sems.at[1]),
        pltpu.make_async_copy(control_ref.at[0], ends.at[0], sems.at[2]),
        pltpu.make_async_copy(control_ref.at[rows - 1], ends.at[1], sems.at[3]),
    ]
    for load in loads:
        load.start()
    greet()
    for load in loads:
        load.wait()
    sides[0] = tiles[0, :, 0, :]
    sides[1] = tiles[1, :, 7, :]
    low, high = pl.ds(0, EDGE), pl.ds(rows + EDGE, EDGE)
    first, last = pl.ds(0, EDGE), pl.ds(rows - EDGE, EDGE)
    start_halo, wait_halo = exchange({
        (1, 0): (ends.at[1], north_ref),
        (-1, 0): (ends.at[0], south_ref),
        (0, 1): (sides.at[1], west_ref.at[pl.ds(EDGE, rows), :]),
        (0, -1): (sides.at[0], east_ref.at[pl.ds(EDGE, rows), :]),
        (1, 1): (sides.at[1, last, :], west_ref.at[low, :]),
        (1, -1): (sides.at[0, last, :], east_ref.at[low, :]),
        (-1, 1): (sides.at[1, first, :], west_ref.at[high, :]),
        (-1, -1): (sides.at[0, first, :], east_ref.at[high, :]),
    }, send_sems, recv_sems)
    start_halo()
    for k in range(9):
        g = combined(corr_ref, jac_ref, k)
        hi, lo = split(g)
        g_both[k * 128:(k + 1) * 128, 0:128] = hi
        g_both[k * 128:(k + 1) * 128, 128:256] = lo
        hi, lo = split(g.T)
        for half in range(2):
            gt_hi[half * 128:(half + 1) * 128, k * 128:(k + 1) * 128] = hi
            gt_lo[half * 128:(half + 1) * 128, k * 128:(k + 1) * 128] = lo
    wait_halo()


def back_kernel(out_n, out_s, out_w, out_e, got_n, got_s, got_w, got_e, nw, ne, sw, se, send_sems, recv_sems):
    cols = out_n.shape[0] - 2 * EDGE
    middle, low, high = pl.ds(EDGE, cols), pl.ds(0, EDGE), pl.ds(cols + EDGE, EDGE)
    greet()
    start_edges, wait_edges = exchange({
        (1, 0): (out_s.at[middle, :], got_n),
        (-1, 0): (out_n.at[middle, :], got_s),
        (0, 1): (out_e, got_w),
        (0, -1): (out_w, got_e),
        (1, 1): (out_s.at[high, :], nw),
        (1, -1): (out_s.at[low, :], ne),
        (-1, 1): (out_n.at[high, :], sw),
        (-1, -1): (out_n.at[low, :], se),
    }, send_sems, recv_sems)
    start_edges()
    wait_edges()


def finish_kernel(north_ref, south_ref, west_ref, east_ref, nw_ref, ne_ref, sw_ref, se_ref, grad_in,
                  grad_ref, line_n, line_s, tile_w, tile_e, sems):
    rows, cols, _ = grad_in.shape
    inner = pl.ds(1, rows - 2)
    ends = ((grad_ref.at[0], line_n), (grad_ref.at[rows - 1], line_s),
            (grad_ref.at[inner, pl.ds(0, 8), :], tile_w), (grad_ref.at[inner, pl.ds(cols - 8, 8), :], tile_e))
    loads = [pltpu.make_async_copy(far, near, sems.at[i]) for i, (far, near) in enumerate(ends)]
    for copy in loads:
        copy.start()
    for copy in loads:
        copy.wait()
    line_n[...] += north_ref[...]
    line_s[...] += south_ref[...]
    line_n[0:1, :] += west_ref[0:1, :] + nw_ref[0:1, :]
    line_n[cols - 1:cols, :] += east_ref[0:1, :] + ne_ref[7:8, :]
    line_s[0:1, :] += west_ref[rows - 1:rows, :] + sw_ref[0:1, :]
    line_s[cols - 1:cols, :] += east_ref[rows - 1:rows, :] + se_ref[7:8, :]

    flat_w = tile_w.reshape((rows - 2) * 8, 128)
    flat_e = tile_e.reshape((rows - 2) * 8, 128)
    flat_w[pl.ds(0, rows - 2, stride=8), :] += west_ref[1:rows - 1, :]
    flat_e[pl.ds(7, rows - 2, stride=8), :] += east_ref[1:rows - 1, :]
    stores = [pltpu.make_async_copy(near, far, sems.at[i]) for i, (far, near) in enumerate(ends)]
    for copy in stores:
        copy.start()
    for copy in stores:
        copy.wait()


def body(control, corr_blocks, jacobian, obs_values, obs_count, obs_col, obs_frac, obs_rinv):
    n_devices = lax.axis_size("lat") * lax.axis_size("lon")
    rows, cols, levels = control.shape
    channels = jacobian.shape[1]
    slots = obs_col.shape[1]
    pitch = cols + 2 * EDGE
    vmem = pl.BlockSpec(memory_space=pltpu.VMEM)
    smem = pl.BlockSpec(memory_space=pltpu.SMEM)
    hbm = pl.BlockSpec(memory_space=pl.ANY)

    def to_owners(x):
        blocks = x.reshape(n_devices, CAP, channels)
        return lax.all_to_all(blocks, ("lat", "lon"), split_axis=0, concat_axis=0, tiled=True).reshape(slots, channels)

    observed = to_owners(obs_values)

    def struct(count):
        return jax.ShapeDtypeStruct((count, levels), F32)

    north, south, west, east, g_both, gt_hi, gt_lo = pl.pallas_call(
        front_kernel,
        out_shape=[struct(cols), struct(cols), struct(rows + 2 * EDGE), struct(rows + 2 * EDGE),
                   jax.ShapeDtypeStruct((9 * levels, 2 * channels), BF16),
                   jax.ShapeDtypeStruct((2 * channels, 9 * levels), BF16),
                   jax.ShapeDtypeStruct((2 * channels, 9 * levels), BF16)],
        in_specs=[hbm, vmem, vmem],
        out_specs=[vmem] * 7,
        scratch_shapes=[
            pltpu.VMEM((2, rows, 8, levels), F32),
            pltpu.VMEM((2, cols, levels), F32),
            pltpu.VMEM((2, rows, levels), F32),
            pltpu.SemaphoreType.DMA((8,)),
            pltpu.SemaphoreType.DMA((8,)),
            pltpu.SemaphoreType.DMA((4,)),
        ],
        compiler_params=pltpu.CompilerParams(collective_id=0, has_side_effects=True, vmem_limit_bytes=56 * 2**20),
        name="front",
    )(control, corr_blocks, jacobian)

    chunk_slots = math.gcd(slots, 512)
    limit = pltpu.CompilerParams(vmem_limit_bytes=56 * 2**20)
    weighted, rounded = pl.pallas_call(
        functools.partial(forward_kernel, pitch, chunk_slots),
        out_shape=[jax.ShapeDtypeStruct((slots, channels), F32), jax.ShapeDtypeStruct((slots, channels), BF16)],
        in_specs=[smem, smem] + [vmem] * 8 + [hbm],
        out_specs=[vmem, vmem],
        scratch_shapes=[
            pltpu.VMEM((rows + 2, pitch, levels), F32),
            pltpu.VMEM((ODD * 8, levels), F32),
            pltpu.VMEM((ODD * 8, levels), F32),
            pltpu.VMEM((chunk_slots, levels), F32),
            pltpu.VMEM((chunk_slots, levels), F32),
            pltpu.VMEM((2 * chunk_slots, 9 * levels), BF16),
            pltpu.SemaphoreType.DMA,
        ],
        compiler_params=limit,
        cost_estimate=pl.CostEstimate(flops=2 * slots * 1152 * 512, bytes_accessed=40 * 2**20, transcendentals=0),
        name="forward",
    )(obs_col, obs_count, obs_frac, obs_rinv, observed, g_both, north, south, west, east, control)

    returned = to_owners(rounded)

    gradient, out_n, out_s, out_w, out_e = pl.pallas_call(
        functools.partial(adjoint_kernel, pitch, chunk_slots),
        out_shape=[
            jax.ShapeDtypeStruct(control.shape, F32),
            jax.ShapeDtypeStruct((pitch, levels), F32),
            jax.ShapeDtypeStruct((pitch, levels), F32),
            jax.ShapeDtypeStruct((rows, levels), F32),
            jax.ShapeDtypeStruct((rows, levels), F32),
        ],
        in_specs=[smem] + [vmem] * 4 + [hbm],
        out_specs=[hbm] + [vmem] * 4,
        scratch_shapes=[
            pltpu.VMEM((rows + 2, pitch, levels), F32),
            pltpu.VMEM((ODD * 8, levels), F32),
            pltpu.VMEM((ODD * 8, levels), F32),
            pltpu.VMEM((chunk_slots, levels), F32),
            pltpu.VMEM((chunk_slots, levels), F32),
            pltpu.VMEM((chunk_slots, 9 * levels), F32),
            pltpu.SemaphoreType.DMA,
        ],
        compiler_params=limit,
        cost_estimate=pl.CostEstimate(flops=2 * slots * 1152 * 512, bytes_accessed=60 * 2**20, transcendentals=0),
        name="adjoint",
    )(obs_col, obs_frac, gt_hi, gt_lo, weighted, control)

    got = pl.pallas_call(
        back_kernel,
        out_shape=[struct(cols), struct(cols), struct(rows), struct(rows)] + [struct(EDGE)] * 4,
        in_specs=[vmem] * 4,
        out_specs=[vmem] * 8,
        scratch_shapes=[
            pltpu.SemaphoreType.DMA((8,)),
            pltpu.SemaphoreType.DMA((8,)),
        ],
        compiler_params=pltpu.CompilerParams(collective_id=1, has_side_effects=True),
        name="back",
    )(out_n, out_s, out_w, out_e)
    gradient = pl.pallas_call(
        finish_kernel,
        out_shape=jax.ShapeDtypeStruct(control.shape, F32),
        in_specs=[vmem] * 8 + [hbm],
        out_specs=hbm,
        scratch_shapes=[
            pltpu.VMEM((cols, levels), F32),
            pltpu.VMEM((cols, levels), F32),
            pltpu.VMEM((rows - 2, 8, levels), F32),
            pltpu.VMEM((rows - 2, 8, levels), F32),
            pltpu.SemaphoreType.DMA((4,)),
        ],
        input_output_aliases={8: 0},
        name="finish",
    )(*got, gradient)
    return (gradient, returned)


def solution(mesh):
    in_specs = (
        P("lat", "lon", None),
        P(),
        P(),
        P(("lat", "lon"), None),
        P(("lat", "lon"), None),
        P(("lat", "lon"), None),
        P(("lat", "lon"), None, None),
        P(("lat", "lon"), None),
    )
    out_specs = (P("lat", "lon", None), P(("lat", "lon"), None))
    return jax.shard_map(body, mesh=mesh, in_specs=in_specs, out_specs=out_specs, check_vma=False)
```
